32 devices in a mesh: ta: 4 (over z), af: 8 (over y, x, core).
Axes of the slice: x: 2, y: 2, z: 4, core: 2. Of those that a mesh axis runs over, the one named last changes fastest.
Arguments:
- velocity: float32 [16, 512, 128, 128], P(None, ('ta', 'af')), may hold values from -14 to 14
- initial_basis: float32 [512, 64], replicated, may hold values from -6 to 6
Outputs:
- core: float32 [16, 128, 64, 128], P('ta', 'af')
The draws below stay inside these ranges and needn't reach their ends.
All inputs are finite; a program needn't handle non-finite values.
Results may differ from the reference program's by a relative error of at most 0.00017.
Values sent between devices are 32-bit elements; how exact they have to be, the bound alone decides.
No kernel may reach another device: no remote copies, remote signals or barrier semaphores. Data moves between devices by JAX's collectives and lax.ppermute only.
A program may use at most 64 MiB of HBM per device.

```python
import math
import jax
import jax.numpy as jnp
from jax import lax

Z = 512
X = 128
Y = 128
K = 64
F = 16
ITERS = 3


def draw_velocity(key, part):
    key_scale = jax.random.fold_in(key, 11)
    key_noise = jax.random.fold_in(key, 23)
    log_scale = jax.random.uniform(key_scale, (Z,), jnp.float32, math.log(0.5), math.log(2.0))
    plane_scale = jnp.exp(log_scale)[None, :, None, None]
    fluctuation = jnp.clip(jax.random.normal(key_noise, (F, Z, X, Y), jnp.float32), -6.0, 6.0)
    return fluctuation * plane_scale


def gaussian(stream_key, extent, deviation, reach, held_as=jnp.bfloat16):
    return jnp.clip(deviation * jax.random.normal(stream_key, extent, jnp.float32), -reach, reach).astype(held_as)


def setup_inputs(seed: int = 0) -> dict:
    keys = jax.random.split(jax.random.key(seed), 3)
    velocity = draw_velocity(jax.random.fold_in(keys[2], 71), 0)
    initial_basis = gaussian(keys[1], (Z, K), 1.0, 6.0, jnp.float32)
    return dict(velocity=velocity, initial_basis=initial_basis)


def orthonormal(product):
    lower = jnp.linalg.cholesky(jnp.dot(product.T.astype(jnp.float32), product.astype(jnp.float32), precision=lax.Precision.HIGHEST, preferred_element_type=jnp.float32))
    return jax.scipy.linalg.solve_triangular(lower, product.T, lower=True).T

def reference(velocity, initial_basis):

    def accumulate(running, one_frame):
        matrix = one_frame.reshape(Z, X * Y)
        return (running + jnp.dot(matrix.astype(jnp.float32), matrix.T.astype(jnp.float32), precision=lax.Precision.HIGHEST, preferred_element_type=jnp.float32), None)
    gram_matrix, unused = lax.scan(accumulate, jnp.zeros((Z, Z), jnp.float32), velocity)
    subspace = initial_basis
    for iteration in range(ITERS):
        subspace = orthonormal(jnp.dot(gram_matrix.astype(jnp.float32), subspace.astype(jnp.float32), precision=lax.Precision.HIGHEST, preferred_element_type=jnp.float32))

    def project(one_frame):
        return jnp.einsum('zxy,zk->xky', one_frame.astype(jnp.float32), subspace.astype(jnp.float32), precision=lax.Precision.HIGHEST, preferred_element_type=jnp.float32)
    return lax.map(project, velocity)
```

```python
import functools

import jax
import jax.numpy as jnp
from jax import lax
from jax.experimental import pallas as pl
from jax.experimental.pallas import tpu as pltpu
from jax.sharding import PartitionSpec as P

ITERS = 3
HIGHEST = lax.Precision.HIGHEST
VMEM_LIMIT = 48 * 1024 * 1024
PIVOTS = 8


def split(matrix):
    high = matrix.astype(jnp.bfloat16)
    low = (matrix - high.astype(jnp.float32)).astype(jnp.bfloat16)
    return high, low


def nn(left, right, precision=None):
    return lax.dot_general(
        left, right, (((1,), (0,)), ((), ())), precision=precision,
        preferred_element_type=jnp.float32,
    )


def nt(left, right, precision=None):
    return lax.dot_general(
        left, right, (((1,), (1,)), ((), ())), precision=precision,
        preferred_element_type=jnp.float32,
    )


def largest_step(extent, most):
    step = min(extent, most)
    while extent % step:
        step -= 1
    return step


def plane_matrix(block_ref, first, count):
    sources, _, planes, cells_y = block_ref.shape
    return jnp.concatenate(
        [block_ref[:, first + i].reshape(sources * planes, cells_y) for i in range(count)], axis=1
    )


def gram_kernel(block_ref, before_ref, total_ref):
    @pl.when(pl.program_id(0) == 0)
    def _():
        total_ref[...] = before_ref[...]

    high, low = split(plane_matrix(block_ref, 0, block_ref.shape[1]))
    left = jnp.concatenate([high, high], axis=1)
    right = jnp.concatenate([high, low * jnp.bfloat16(2)], axis=1)
    total_ref[...] += nt(left, right)


def gram_add(block, before):
    sources, cells_x, planes, cells_y = block.shape
    planes_total = sources * planes
    step = largest_step(cells_x, 4)
    whole = pl.BlockSpec((planes_total, planes_total), lambda i: (0, 0))
    return pl.pallas_call(
        gram_kernel,
        grid=(cells_x // step,),
        in_specs=[pl.BlockSpec((sources, step, planes, cells_y), lambda i: (0, i, 0, 0)), whole],
        out_specs=whole,
        out_shape=jax.ShapeDtypeStruct((planes_total, planes_total), jnp.float32),
        compiler_params=pltpu.CompilerParams(vmem_limit_bytes=VMEM_LIMIT),
        name="gram_add",
    )(block, before)


def inverse_cholesky(matrix):
    size = matrix.shape[0]
    rows = lax.broadcasted_iota(jnp.int32, (size, 2 * size), 0)
    lanes = lax.broadcasted_iota(jnp.int32, (size, size), 1)
    identity = (lanes == rows[:, :size]).astype(jnp.float32)
    work = jnp.concatenate([matrix, identity], axis=1)
    scale = jnp.zeros_like(work)
    for first in range(0, size, PIVOTS):
        columns = [
            jnp.broadcast_to(work[:, first + i : first + i + 1], work.shape) for i in range(PIVOTS)
        ]
        for i in range(PIVOTS):
            j = first + i
            pivot = columns[i][j : j + 1]
            scale = jnp.where(rows == j, lax.rsqrt(pivot), scale)
            factor = jnp.where(rows > j, columns[i] * (1.0 / pivot), 0.0)
            work = work - factor * work[j : j + 1]
            for m in range(i + 1, PIVOTS):
                columns[m] = columns[m] - factor * columns[m][j : j + 1]
    return (work * scale)[:, size:]


def iterate_kernel(total_ref, basis_ref, out_ref):
    total = total_ref[...]
    gram = 0.5 * (total + total.T)
    subspace = basis_ref[...]
    for _ in range(ITERS):
        product = nn(subspace, gram, HIGHEST)
        inverse = inverse_cholesky(nt(product, product, HIGHEST))
        subspace = nn(inverse, product, HIGHEST)
    out_ref[...] = subspace


def iterate(total, basis_t):
    return pl.pallas_call(
        iterate_kernel,
        out_shape=jax.ShapeDtypeStruct(basis_t.shape, jnp.float32),
        compiler_params=pltpu.CompilerParams(vmem_limit_bytes=VMEM_LIMIT),
        name="iterate",
    )(total, basis_t)


def project_kernel(count, subspace_ref, *refs):
    blocks, out_ref = refs[:count], refs[count]
    rank = subspace_ref.shape[0]
    basis_high, basis_low = split(subspace_ref[...])
    both = jnp.concatenate([basis_high, basis_low], axis=0)
    for j, block_ref in enumerate(blocks):
        step, cells_y = block_ref.shape[1], block_ref.shape[3]
        high, low = split(plane_matrix(block_ref, 0, step))
        main = nn(both, high)
        result = main[:rank] + (main[rank:] + nn(basis_high, low))
        for i in range(step):
            out_ref[j, i] = result[:, i * cells_y : (i + 1) * cells_y]


def project(subspace, blocks):
    sources, cells_x, planes, cells_y = blocks[0].shape
    rank = subspace.shape[0]
    step = largest_step(cells_x, 2)
    return pl.pallas_call(
        functools.partial(project_kernel, len(blocks)),
        grid=(cells_x // step,),
        in_specs=[pl.BlockSpec(subspace.shape, lambda i: (0, 0))]
        + [pl.BlockSpec((sources, step, planes, cells_y), lambda i: (0, i, 0, 0))] * len(blocks),
        out_specs=pl.BlockSpec((len(blocks), step, rank, cells_y), lambda i: (0, i, 0, 0)),
        out_shape=jax.ShapeDtypeStruct((len(blocks), cells_x, rank, cells_y), jnp.float32),
        compiler_params=pltpu.CompilerParams(vmem_limit_bytes=VMEM_LIMIT),
        name="project",
    )(subspace, *blocks)


def sum_over_devices(total):
    groups_af = lax.axis_size("af")
    groups_ta = lax.axis_size("ta")
    rows = total.shape[0] // groups_af
    parts = lax.all_to_all(
        total.reshape(groups_af, rows, total.shape[1]), "af", split_axis=0, concat_axis=0, tiled=True
    )
    mine = parts.sum(axis=0)
    summed = mine
    for distance in range(1, groups_ta):
        summed = summed + lax.ppermute(
            mine, "ta", [(i, (i + distance) % groups_ta) for i in range(groups_ta)]
        )
    spread = jnp.broadcast_to(summed[None], (groups_af,) + summed.shape)
    return lax.all_to_all(spread, "af", split_axis=0, concat_axis=0, tiled=True).reshape(total.shape)


def local(velocity, initial_basis):
    groups_ta = lax.axis_size("ta")
    groups_af = lax.axis_size("af")
    devices = groups_ta * groups_af
    frames, planes, cells_x, cells_y = velocity.shape
    planes_total = initial_basis.shape[0]
    block_frames, block_x = frames // groups_ta, cells_x // groups_af
    split_up = velocity.reshape(groups_ta, block_frames, planes, groups_af, block_x, cells_y)
    blocks = []
    total = jnp.zeros((planes_total, planes_total), jnp.float32)
    for j in range(block_frames):
        outgoing = split_up[:, j].transpose(0, 2, 3, 1, 4)
        outgoing = outgoing.reshape(devices, block_x, planes, cells_y)
        block = lax.all_to_all(outgoing, ("ta", "af"), split_axis=0, concat_axis=0, tiled=True)
        if planes % 8:
            block = block.transpose(1, 0, 2, 3).reshape(1, block_x, planes_total, cells_y)
        blocks.append(block)
        total = gram_add(block, total)
    total = sum_over_devices(total)
    subspace = iterate(total, initial_basis.T)
    return project(subspace, blocks)


def solution(mesh):
    placed = (P(None, ("ta", "af"), None, None), P())
    return jax.shard_map(
        local, mesh=mesh, in_specs=placed, out_specs=P("ta", "af", None, None), check_vma=False
    )
```

```python
import functools
import math

import jax
import jax.numpy as jnp
from jax import lax
from jax.experimental import pallas as pl
from jax.experimental.pallas import tpu as pltpu
from jax.sharding import PartitionSpec as P

ITERS = 3
HIGHEST = lax.Precision.HIGHEST
VMEM_LIMIT = 48 * 1024 * 1024
PIVOTS = 8
GRAM_CELLS = 4
PROJECT_CELLS = 8


def split(matrix):
    high = matrix.astype(jnp.bfloat16)
    low = (matrix - high.astype(jnp.float32)).astype(jnp.bfloat16)
    return high, low


def nn(left, right, precision=None):
    return lax.dot_general(
        left, right, (((1,), (0,)), ((), ())), precision=precision,
        preferred_element_type=jnp.float32,
    )


def nt(left, right, precision=None):
    return lax.dot_general(
        left, right, (((1,), (1,)), ((), ())), precision=precision,
        preferred_element_type=jnp.float32,
    )


def largest_step(extent, most):
    step = min(extent, most)
    while extent % step:
        step -= 1
    return step


def cell_matrix(block_ref):
    sources, cells, planes, cells_y = block_ref.shape
    return jnp.concatenate(
        [block_ref[:, i].reshape(sources * planes, cells_y) for i in range(cells)], axis=1
    )


def add_products(block_ref, total_ref):
    high, low = split(cell_matrix(block_ref))
    left = jnp.concatenate([high, high], axis=1)
    right = jnp.concatenate([high, low * jnp.bfloat16(2)], axis=1)
    total_ref[...] += nt(left, right)


def gram_kernel(block_ref, total_ref):
    @pl.when(pl.program_id(0) == 0)
    def _():
        total_ref[...] = jnp.zeros_like(total_ref)

    add_products(block_ref, total_ref)


def gram_more_kernel(block_ref, before_ref, total_ref):
    @pl.when(pl.program_id(0) == 0)
    def _():
        total_ref[...] = before_ref[...]

    add_products(block_ref, total_ref)


def lower_blocks(count):
    return [(i, j) for i in range(count) for j in range(i + 1)]


def gram_pack_kernel(block_ref, before_ref, packed_ref, total_ref):
    gram_more_kernel(block_ref, before_ref, total_ref)

    @pl.when(pl.program_id(0) == pl.num_programs(0) - 1)
    def _():
        group = packed_ref.shape[1]
        blocks = lower_blocks(total_ref.shape[0] // group)
        for n, (i, j) in enumerate(blocks):
            block = total_ref[i * group : (i + 1) * group, j * group : (j + 1) * group]
            mirrored = total_ref[j * group : (j + 1) * group, i * group : (i + 1) * group]
            packed_ref[n * group : (n + 1) * group, :] = 0.5 * (block + mirrored.T)
        rest = packed_ref.shape[0] - len(blocks) * group
        if rest:
            packed_ref[len(blocks) * group :, :] = jnp.zeros((rest, group), jnp.float32)


def gram(block, before, parts=None):
    sources, cells, planes, cells_y = block.shape
    planes_total = sources * planes
    step = largest_step(cells, GRAM_CELLS)
    square = (planes_total, planes_total)
    whole = pl.BlockSpec(square, lambda i: (0, 0))
    in_specs = [pl.BlockSpec((sources, step, planes, cells_y), lambda i: (0, i, 0, 0))]
    operands = [block]
    kernel, out_shape, scratch = gram_kernel, square, []
    if before is not None:
        in_specs.append(whole)
        operands.append(before)
        kernel = gram_more_kernel
    if parts is not None:
        group = planes_total // largest_step(planes_total, planes_total // 128)
        rows = len(lower_blocks(planes_total // group)) * group
        out_shape = (rows + -rows % (8 * parts), group)
        kernel, scratch = gram_pack_kernel, [pltpu.VMEM(square, jnp.float32)]
    return pl.pallas_call(
        kernel,
        grid=(cells // step,),
        in_specs=in_specs,
        out_specs=pl.BlockSpec(out_shape, lambda i: (0, 0)),
        out_shape=jax.ShapeDtypeStruct(out_shape, jnp.float32),
        scratch_shapes=scratch,
        compiler_params=pltpu.CompilerParams(vmem_limit_bytes=VMEM_LIMIT),
        name="gram",
    )(*operands)


def inverse_cholesky(matrix):
    size = matrix.shape[0]
    rows = lax.broadcasted_iota(jnp.int32, (size, 2 * size), 0)
    lanes = lax.broadcasted_iota(jnp.int32, (size, size), 1)
    identity = (lanes == rows[:, :size]).astype(jnp.float32)
    work = jnp.concatenate([matrix, identity], axis=1)
    scale = jnp.zeros_like(work)
    for first in range(0, size, PIVOTS):
        columns = [
            jnp.broadcast_to(work[:, first + i : first + i + 1], work.shape) for i in range(PIVOTS)
        ]
        for i in range(PIVOTS):
            j = first + i
            pivot = columns[i][j : j + 1]
            scale = jnp.where(rows == j, lax.rsqrt(pivot), scale)
            factor = jnp.where(rows > j, columns[i] * (1.0 / pivot), 0.0)
            work = work - factor * work[j : j + 1]
            for m in range(i + 1, PIVOTS):
                columns[m] = columns[m] - factor * columns[m][j : j + 1]
    return (work * scale)[:, size:]


def iterate_kernel(packed_ref, basis_ref, out_ref, gram_ref):
    group = packed_ref.shape[1]
    for n, (i, j) in enumerate(lower_blocks(gram_ref.shape[0] // group)):
        block = packed_ref[n * group : (n + 1) * group, :]
        gram_ref[i * group : (i + 1) * group, j * group : (j + 1) * group] = block
        if i != j:
            gram_ref[j * group : (j + 1) * group, i * group : (i + 1) * group] = block.T
    matrix = gram_ref[...]
    subspace = basis_ref[...]
    for _ in range(ITERS):
        product = nn(subspace, matrix, HIGHEST)
        inverse = inverse_cholesky(nt(product, product, HIGHEST))
        subspace = nn(inverse, product, HIGHEST)
    out_ref[...] = subspace


def iterate(packed, basis_t):
    planes_total = basis_t.shape[1]
    return pl.pallas_call(
        iterate_kernel,
        out_shape=jax.ShapeDtypeStruct(basis_t.shape, jnp.float32),
        scratch_shapes=[pltpu.VMEM((planes_total, planes_total), jnp.float32)],
        compiler_params=pltpu.CompilerParams(vmem_limit_bytes=VMEM_LIMIT),
        name="iterate",
    )(packed, basis_t)


def project_kernel(steps, subspace_ref, *refs):
    blocks, out_ref = refs[:-1], refs[-1]
    rank = subspace_ref.shape[0]
    basis_high, basis_low = split(subspace_ref[...])
    both = jnp.concatenate([basis_high, basis_low], axis=0)
    first = 0
    for count, block_ref in zip(steps, blocks):

        @pl.when((pl.program_id(0) >= first) & (pl.program_id(0) < first + count))
        def _(block_ref=block_ref):
            cells, cells_y = block_ref.shape[1], block_ref.shape[3]
            high, low = split(cell_matrix(block_ref))
            main = nn(both, high)
            result = main[:rank] + (main[rank:] + nn(basis_high, low))
            for i in range(cells):
                out_ref[i] = result[:, i * cells_y : (i + 1) * cells_y]

        first += count


def project(subspace, blocks):
    sources, _, planes, cells_y = blocks[0].shape
    rank = subspace.shape[0]
    cells = [block.shape[1] for block in blocks]
    step = largest_step(math.gcd(*cells), PROJECT_CELLS)
    steps = [count // step for count in cells]
    in_specs = [pl.BlockSpec(subspace.shape, lambda i: (0, 0))]
    for n, count in enumerate(steps):
        first = sum(steps[:n])
        in_specs.append(
            pl.BlockSpec(
                (sources, step, planes, cells_y),
                lambda i, first=first, count=count: (0, jnp.clip(i - first, 0, count - 1), 0, 0),
            )
        )
    return pl.pallas_call(
        functools.partial(project_kernel, steps),
        grid=(sum(steps),),
        in_specs=in_specs,
        out_specs=pl.BlockSpec((step, rank, cells_y), lambda i: (i, 0, 0)),
        out_shape=jax.ShapeDtypeStruct((sum(cells), rank, cells_y), jnp.float32),
        compiler_params=pltpu.CompilerParams(vmem_limit_bytes=VMEM_LIMIT),
        name="project",
    )(subspace, *blocks)


def sum_over_devices(packed):
    groups_af, groups_ta = lax.axis_size("af"), lax.axis_size("ta")
    rows = packed.shape[0] // groups_af
    parts = lax.all_to_all(
        packed.reshape(groups_af, rows, packed.shape[1]), "af", split_axis=0, concat_axis=0, tiled=True
    )
    mine = parts.sum(axis=0)
    summed = mine
    for distance in range(1, groups_ta):
        summed = summed + lax.ppermute(
            mine, "ta", [(i, (i + distance) % groups_ta) for i in range(groups_ta)]
        )
    spread = jnp.broadcast_to(summed[None], (groups_af,) + summed.shape)
    return lax.all_to_all(spread, "af", split_axis=0, concat_axis=0, tiled=True).reshape(packed.shape)


def arrange_kernel(in_ref, out_ref):
    for x in range(in_ref.shape[3]):
        for target in range(in_ref.shape[2]):
            out_ref[target, x] = in_ref[0, :, target, x]


def outgoing(velocity, first, count):
    groups_ta, groups_af = lax.axis_size("ta"), lax.axis_size("af")
    frames, planes, cells_x, cells_y = velocity.shape
    block_frames, block_x = frames // groups_ta, cells_x // groups_af
    part = cell_step(block_x)
    if planes % 8 or part % 8:
        ordered = velocity.reshape(groups_ta, block_frames, planes, groups_af, block_x, cells_y)
        ordered = ordered.transpose(0, 3, 1, 4, 2, 5)
        ordered = ordered.reshape(groups_ta * groups_af, -1, planes, cells_y)
        return ordered[:, first : first + count]
    parts_x, start = block_x // part, first // part

    def source(group, i):
        frame = group * block_frames + (start + i) // parts_x
        return frame, 0, 0, lax.rem(start + i, parts_x), 0

    return pl.pallas_call(
        arrange_kernel,
        grid=(groups_ta, count // part),
        in_specs=[pl.BlockSpec((1, planes, groups_af, part, cells_y), source)],
        out_specs=pl.BlockSpec((groups_af, part, planes, cells_y), lambda group, i: (group, i, 0, 0)),
        out_shape=jax.ShapeDtypeStruct(
            (groups_ta * groups_af, count, planes, cells_y), jnp.float32
        ),
        compiler_params=pltpu.CompilerParams(vmem_limit_bytes=VMEM_LIMIT),
        name="arrange",
    )(velocity.reshape(frames, planes, groups_af, block_x, cells_y))


def cell_step(block_x):
    return 8 if block_x % 8 == 0 else block_x


def local(velocity, initial_basis):
    groups_ta, groups_af = lax.axis_size("ta"), lax.axis_size("af")
    frames, planes, cells_x, cells_y = velocity.shape
    block_frames, block_x = frames // groups_ta, cells_x // groups_af
    cells, part = block_frames * block_x, cell_step(block_x)
    edge = min(part, cells // 3)
    blocks = []
    for first, count in ((0, edge), (edge, cells - 2 * edge), (cells - edge, edge)):
        block = outgoing(velocity, first, count)
        if blocks:
            block, blocks[-1] = lax.optimization_barrier((block, blocks[-1]))
        block = lax.all_to_all(block, ("ta", "af"), split_axis=0, concat_axis=0, tiled=True)
        blocks.append(block)
    if planes % 8:
        blocks = [
            block.transpose(1, 0, 2, 3).reshape(1, block.shape[1], -1, cells_y) for block in blocks
        ]
    total = gram(blocks[0], None)
    total = gram(blocks[1], total)
    packed = sum_over_devices(gram(blocks[2], total, groups_af))
    subspace = iterate(packed, initial_basis.T)
    core = project(subspace, blocks)
    return core.reshape(block_frames, block_x, core.shape[1], cells_y)


def solution(mesh):
    placed = (P(None, ("ta", "af"), None, None), P())
    return jax.shard_map(
        local, mesh=mesh, in_specs=placed, out_specs=P("ta", "af", None, None), check_vma=False
    )
```

```python
import functools

import jax
import jax.numpy as jnp
from jax import lax
from jax.experimental import pallas as pl
from jax.experimental.pallas import tpu as pltpu
from jax.sharding import PartitionSpec as P

ITERS = 3
HIGHEST = lax.Precision.HIGHEST
VMEM_LIMIT = 48 * 1024 * 1024
PIVOTS = 8
GRAM_CELLS = 4
PROJECT_CELLS = 8


def split(matrix):
    high = matrix.astype(jnp.bfloat16)
    low = (matrix - high.astype(jnp.float32)).astype(jnp.bfloat16)
    return high, low


def nn(left, right, precision=None):
    return lax.dot_general(
        left, right, (((1,), (0,)), ((), ())), precision=precision,
        preferred_element_type=jnp.float32,
    )


def nt(left, right, precision=None):
    return lax.dot_general(
        left, right, (((1,), (1,)), ((), ())), precision=precision,
        preferred_element_type=jnp.float32,
    )


def largest_step(extent, most):
    step = min(extent, most)
    while extent % step:
        step -= 1
    return step


def cell_matrix(block_ref):
    sources, cells, planes, cells_y = block_ref.shape
    return jnp.concatenate(
        [block_ref[:, i].reshape(sources * planes, cells_y) for i in range(cells)], axis=1
    )


def add_products(block_ref, total_ref):
    high, low = split(cell_matrix(block_ref))
    left = jnp.concatenate([high, high], axis=1)
    right = jnp.concatenate([high, low * jnp.bfloat16(2)], axis=1)
    total_ref[...] += nt(left, right)


def gram_kernel(block_ref, total_ref):
    @pl.when(pl.program_id(0) == 0)
    def _():
        total_ref[...] = jnp.zeros_like(total_ref)

    add_products(block_ref, total_ref)


def gram_more_kernel(block_ref, before_ref, total_ref):
    @pl.when(pl.program_id(0) == 0)
    def _():
        total_ref[...] = before_ref[...]

    add_products(block_ref, total_ref)


def lower_blocks(count):
    return [(i, j) for i in range(count) for j in range(i + 1)]


def gram_pack_kernel(block_ref, before_ref, packed_ref, total_ref):
    gram_more_kernel(block_ref, before_ref, total_ref)

    @pl.when(pl.program_id(0) == pl.num_programs(0) - 1)
    def _():
        group = packed_ref.shape[1]
        blocks = lower_blocks(total_ref.shape[0] // group)
        for n, (i, j) in enumerate(blocks):
            block = total_ref[i * group : (i + 1) * group, j * group : (j + 1) * group]
            mirrored = total_ref[j * group : (j + 1) * group, i * group : (i + 1) * group]
            packed_ref[n * group : (n + 1) * group, :] = 0.5 * (block + mirrored.T)
        rest = packed_ref.shape[0] - len(blocks) * group
        if rest:
            packed_ref[len(blocks) * group :, :] = jnp.zeros((rest, group), jnp.float32)


def gram(block, before, parts=None):
    sources, cells, planes, cells_y = block.shape
    planes_total = sources * planes
    step = largest_step(cells, GRAM_CELLS)
    square = (planes_total, planes_total)
    whole = pl.BlockSpec(square, lambda i: (0, 0))
    in_specs = [pl.BlockSpec((sources, step, planes, cells_y), lambda i: (0, i, 0, 0))]
    operands = [block]
    kernel, out_shape, scratch = gram_kernel, square, []
    if before is not None:
        in_specs.append(whole)
        operands.append(before)
        kernel = gram_more_kernel
    if parts is not None:
        group = planes_total // largest_step(planes_total, planes_total // 128)
        rows = len(lower_blocks(planes_total // group)) * group
        out_shape = (rows + -rows % (8 * parts), group)
        kernel, scratch = gram_pack_kernel, [pltpu.VMEM(square, jnp.float32)]
    return pl.pallas_call(
        kernel,
        grid=(cells // step,),
        in_specs=in_specs,
        out_specs=pl.BlockSpec(out_shape, lambda i: (0, 0)),
        out_shape=jax.ShapeDtypeStruct(out_shape, jnp.float32),
        scratch_shapes=scratch,
        compiler_params=pltpu.CompilerParams(vmem_limit_bytes=VMEM_LIMIT),
        name="gram",
    )(*operands)


def inverse_cholesky(matrix):
    size = matrix.shape[0]
    rows = lax.broadcasted_iota(jnp.int32, (size, 2 * size), 0)
    lanes = lax.broadcasted_iota(jnp.int32, (size, size), 1)
    identity = (lanes == rows[:, :size]).astype(jnp.float32)
    work = jnp.concatenate([matrix, identity], axis=1)
    scale = jnp.zeros_like(work)
    for first in range(0, size, PIVOTS):
        columns = [
            jnp.broadcast_to(work[:, first + i : first + i + 1], work.shape) for i in range(PIVOTS)
        ]
        for i in range(PIVOTS):
            j = first + i
            pivot = columns[i][j : j + 1]
            scale = jnp.where(rows == j, lax.rsqrt(pivot), scale)
            factor = jnp.where(rows > j, columns[i] * (1.0 / pivot), 0.0)
            work = work - factor * work[j : j + 1]
            for m in range(i + 1, PIVOTS):
                columns[m] = columns[m] - factor * columns[m][j : j + 1]
    return (work * scale)[:, size:]


def iterate(matrix, subspace):
    for _ in range(ITERS):
        product = nn(subspace, matrix, HIGHEST)
        inverse = inverse_cholesky(nt(product, product, HIGHEST))
        subspace = nn(inverse, product, HIGHEST)
    return subspace


def unpack(place_ref, pieces, packed_ref, gram_ref):
    rows, group = pieces[0].shape
    for n, piece in enumerate(pieces):
        packed_ref[pl.ds(pl.multiple_of(place_ref[n] * rows, 8), rows), :] = piece[...]
    for n, (i, j) in enumerate(lower_blocks(gram_ref.shape[0] // group)):
        block = packed_ref[n * group : (n + 1) * group, :]
        gram_ref[i * group : (i + 1) * group, j * group : (j + 1) * group] = block
        if i != j:
            gram_ref[j * group : (j + 1) * group, i * group : (i + 1) * group] = block.T


def finish_kernel(pieces_count, blocks_count, *refs):
    place_ref, basis_ref = refs[:2]
    pieces = refs[2 : 2 + pieces_count]
    blocks = refs[2 + pieces_count : 2 + pieces_count + blocks_count]
    rest = refs[2 + pieces_count + blocks_count :]
    out_ref, packed_ref, gram_ref, result_ref, in_sems, out_sems = rest[:1] + rest[1:4] + rest[-2:]
    held = rest[4:-2]
    steps, first = [], 0
    for n, block in enumerate(blocks):
        for start in range(0, block.shape[1], PROJECT_CELLS):
            size = min(PROJECT_CELLS, block.shape[1] - start)
            cells = (slice(None), pl.ds(start, size))
            copy = pltpu.make_async_copy(
                block.at[cells], held[n].at[cells], in_sems.at[len(steps)]
            )
            copy.start()
            steps.append((held[n].at[cells], pl.ds(first, size), copy))
            first += size
    unpack(place_ref, pieces, packed_ref, gram_ref)
    subspace = iterate(gram_ref[...], basis_ref[...])
    rank = subspace.shape[0]
    basis_high, basis_low = split(subspace)
    both = jnp.concatenate([basis_high, basis_low], axis=0)
    copies = []
    for n, (block, cells, arrival) in enumerate(steps):
        arrival.wait()
        cells_y = block.shape[3]
        high, low = split(cell_matrix(block))
        main = nn(both, high)
        result = main[:rank] + (main[rank:] + nn(basis_high, low))
        for i in range(cells.size):
            result_ref[cells.start + i] = result[:, i * cells_y : (i + 1) * cells_y]
        copy = pltpu.make_async_copy(result_ref.at[cells], out_ref.at[cells], out_sems.at[n])
        copy.start()
        copies.append(copy)
    for copy in copies:
        copy.wait()


def finish(places, pieces, basis_t, blocks):
    rank, planes_total = basis_t.shape
    cells = sum(block.shape[1] for block in blocks)
    cells_y = blocks[0].shape[3]
    rows, group = pieces[0].shape
    steps = sum(pl.cdiv(block.shape[1], PROJECT_CELLS) for block in blocks)
    vmem = pl.BlockSpec(memory_space=pltpu.VMEM)
    anywhere = pl.BlockSpec(memory_space=pl.ANY)
    out_shape = (cells, rank, cells_y)
    return pl.pallas_call(
        functools.partial(finish_kernel, len(pieces), len(blocks)),
        in_specs=[pl.BlockSpec(memory_space=pltpu.SMEM), vmem]
        + [vmem] * len(pieces)
        + [anywhere] * len(blocks),
        out_specs=anywhere,
        out_shape=jax.ShapeDtypeStruct(out_shape, jnp.float32),
        scratch_shapes=[
            pltpu.VMEM((rows * len(pieces), group), jnp.float32),
            pltpu.VMEM((planes_total, planes_total), jnp.float32),
            pltpu.VMEM(out_shape, jnp.float32),
        ]
        + [pltpu.VMEM(block.shape, jnp.float32) for block in blocks]
        + [pltpu.SemaphoreType.DMA((steps,)), pltpu.SemaphoreType.DMA((steps,))],
        compiler_params=pltpu.CompilerParams(vmem_limit_bytes=VMEM_LIMIT),
        name="finish",
    )(places, basis_t, *pieces, *blocks)


def toward(i, step, count):
    return i ^ step if count & (count - 1) == 0 else (i + step) % count


def origin(i, step, count):
    return i ^ step if count & (count - 1) == 0 else (i - step) % count


def sum_over_devices(packed):
    groups_af, groups_ta = lax.axis_size("af"), lax.axis_size("ta")
    inner = 2 if groups_af % 2 == 0 else 1
    outer = groups_af // inner
    me = lax.axis_index("af")
    my_outer, my_inner = me // inner, me % inner

    def to_inner(array):
        return lax.ppermute(array, "af", [(i, i ^ 1) for i in range(groups_af)])

    def to_outer(array, step):
        return lax.ppermute(
            array,
            "af",
            [(i, toward(i // inner, step, outer) * inner + i % inner) for i in range(groups_af)],
        )

    def to_ta(array, step):
        return lax.ppermute(array, "ta", [(i, toward(i, step, groups_ta)) for i in range(groups_ta)])

    def pick(array, index):
        return lax.dynamic_index_in_dim(array, index, 0, False)

    def total(arrays):
        return functools.reduce(jnp.add, arrays)

    parts = packed.reshape(inner, -1, packed.shape[1])
    mine = pick(parts, my_inner)
    if inner == 2:
        mine = mine + to_inner(pick(parts, 1 - my_inner))
    parts = mine.reshape(outer, -1, packed.shape[1])
    mine = total(
        [pick(parts, my_outer)]
        + [to_outer(pick(parts, toward(my_outer, k, outer)), k) for k in range(1, outer)]
    )
    mine = total([mine] + [to_ta(mine, k) for k in range(1, groups_ta)])
    pieces = [mine] + [to_outer(mine, k) for k in range(1, outer)]
    places = [my_inner * outer + origin(my_outer, k, outer) for k in range(outer)]
    if inner == 2:
        pieces += [to_inner(piece) for piece in pieces]
        places += [(1 - my_inner) * outer + origin(my_outer, k, outer) for k in range(outer)]
    return pieces, jnp.stack(places).astype(jnp.int32)


def arrange_kernel(in_ref, out_ref):
    for x in range(in_ref.shape[3]):
        for target in range(in_ref.shape[2]):
            out_ref[target, x] = in_ref[0, :, target, x]


def outgoing(velocity, first, count):
    groups_ta, groups_af = lax.axis_size("ta"), lax.axis_size("af")
    frames, planes, cells_x, cells_y = velocity.shape
    block_frames, block_x = frames // groups_ta, cells_x // groups_af
    part = cell_step(block_x)
    if planes % 8 or part % 8:
        ordered = velocity.reshape(groups_ta, block_frames, planes, groups_af, block_x, cells_y)
        ordered = ordered.transpose(0, 3, 1, 4, 2, 5)
        ordered = ordered.reshape(groups_ta * groups_af, -1, planes, cells_y)
        return ordered[:, first : first + count]
    parts_x, start = block_x // part, first // part

    def source(group, i):
        frame = group * block_frames + (start + i) // parts_x
        return frame, 0, 0, lax.rem(start + i, parts_x), 0

    return pl.pallas_call(
        arrange_kernel,
        grid=(groups_ta, count // part),
        in_specs=[pl.BlockSpec((1, planes, groups_af, part, cells_y), source)],
        out_specs=pl.BlockSpec((groups_af, part, planes, cells_y), lambda group, i: (group, i, 0, 0)),
        out_shape=jax.ShapeDtypeStruct(
            (groups_ta * groups_af, count, planes, cells_y), jnp.float32
        ),
        compiler_params=pltpu.CompilerParams(vmem_limit_bytes=VMEM_LIMIT),
        name="arrange",
    )(velocity.reshape(frames, planes, groups_af, block_x, cells_y))


def cell_step(block_x):
    return 8 if block_x % 8 == 0 else block_x


def local(velocity, initial_basis):
    groups_ta, groups_af = lax.axis_size("ta"), lax.axis_size("af")
    frames, planes, cells_x, cells_y = velocity.shape
    block_frames, block_x = frames // groups_ta, cells_x // groups_af
    cells, part = block_frames * block_x, cell_step(block_x)
    edge = min(part, cells // 3)
    blocks = []
    for first, count in ((0, edge), (edge, cells - 2 * edge), (cells - edge, edge)):
        block = outgoing(velocity, first, count)
        if blocks:
            block, blocks[-1] = lax.optimization_barrier((block, blocks[-1]))
        block = lax.all_to_all(block, ("ta", "af"), split_axis=0, concat_axis=0, tiled=True)
        blocks.append(block)
    if planes % 8:
        blocks = [
            block.transpose(1, 0, 2, 3).reshape(1, block.shape[1], -1, cells_y) for block in blocks
        ]
    total = gram(blocks[0], None)
    total = gram(blocks[1], total)
    pieces, places = sum_over_devices(gram(blocks[2], total, groups_af))
    core = finish(places, pieces, initial_basis.T, blocks)
    return core.reshape(block_frames, block_x, core.shape[1], cells_y)


def solution(mesh):
    placed = (P(None, ("ta", "af"), None, None), P())
    return jax.shard_map(
        local, mesh=mesh, in_specs=placed, out_specs=P("ta", "af", None, None), check_vma=False
    )
```

```python
import functools

import jax
import jax.numpy as jnp
from jax import lax
from jax.experimental import pallas as pl
from jax.experimental.pallas import tpu as pltpu
from jax.sharding import PartitionSpec as P

ITERS = 3
HIGHEST = lax.Precision.HIGHEST
MIB = 1024 * 1024
PIVOTS = 16
GRAM_CELLS = 8
PACK_CELLS = 4
PROJECT_CELLS = 8


def split(matrix):
    high = matrix.astype(jnp.bfloat16)
    low = (matrix - high.astype(jnp.float32)).astype(jnp.bfloat16)
    return high, low


def nn(left, right, precision=None):
    return lax.dot_general(
        left, right, (((1,), (0,)), ((), ())), precision=precision,
        preferred_element_type=jnp.float32,
    )


def nt(left, right, precision=None):
    return lax.dot_general(
        left, right, (((1,), (1,)), ((), ())), precision=precision,
        preferred_element_type=jnp.float32,
    )


def largest_step(extent, most):
    step = min(extent, most)
    while extent % step:
        step -= 1
    return step


def cell_matrix(block_ref):
    sources, cells, planes, cells_y = block_ref.shape
    return jnp.concatenate(
        [block_ref[:, i].reshape(sources * planes, cells_y) for i in range(cells)], axis=1
    )


def add_products(block_ref, total_ref):
    high, low = split(cell_matrix(block_ref))
    left = jnp.concatenate([high, high], axis=1)
    right = jnp.concatenate([high, low * jnp.bfloat16(2)], axis=1)
    total_ref[...] += nt(left, right)


def gram_kernel(block_ref, total_ref):
    @pl.when(pl.program_id(0) == 0)
    def _():
        total_ref[...] = jnp.zeros_like(total_ref)

    add_products(block_ref, total_ref)


def gram_more_kernel(block_ref, before_ref, total_ref):
    @pl.when(pl.program_id(0) == 0)
    def _():
        total_ref[...] = before_ref[...]

    add_products(block_ref, total_ref)

    @pl.when(pl.program_id(0) == pl.num_programs(0) - 1)
    def _():
        total = total_ref[...]
        total_ref[...] = 0.5 * (total + total.T)


def lower_blocks(count):
    return [(i, j) for i in range(count) for j in range(i + 1)]


def gram_pack_kernel(place_ref, block_ref, before_ref, *refs):
    parts, total_ref = refs[:-1], refs[-1]
    rows, group = parts[0].shape
    planes_total = before_ref.shape[0]
    half = planes_total // 2 // group * group

    def add(before):
        high, low = split(cell_matrix(block_ref))
        left = jnp.concatenate([high, high, low], axis=1)
        right = jnp.concatenate([high, low, high], axis=1)
        total_ref[:half, :half] = before[:half, :half] + nt(left[:half], right[:half])
        total_ref[half:, :] = before[half:, :] + nt(left[half:], right)

    @pl.when(pl.program_id(0) == 0)
    def _():
        add(before_ref)

    @pl.when(pl.program_id(0) > 0)
    def _():
        add(total_ref)

    blocks = lower_blocks(planes_total // group)
    for place in range(len(parts)):

        @pl.when((pl.program_id(0) == pl.num_programs(0) - 1) & (place_ref[0] == place))
        def _(place=place):
            for k, part_ref in enumerate(parts):
                start = (place + k) % len(parts) * rows
                copy_rows(part_ref, start, blocks, total_ref, group)


def copy_rows(part_ref, start, blocks, total_ref, group):
    done = 0
    while done < part_ref.shape[0]:
        n, skip = divmod(start + done, group)
        size = min(group - skip, part_ref.shape[0] - done)
        if n < len(blocks):
            i, j = blocks[n]
            value = total_ref[
                i * group + skip : i * group + skip + size, j * group : (j + 1) * group
            ]
        else:
            value = jnp.zeros((size, group), jnp.float32)
        part_ref[done : done + size, :] = value
        done += size


def gram(block, before):
    sources, cells, planes, cells_y = block.shape
    planes_total = sources * planes
    step = largest_step(cells, GRAM_CELLS)
    square = (planes_total, planes_total)
    whole = pl.BlockSpec(square, lambda i: (0, 0))
    in_specs = [pl.BlockSpec((sources, step, planes, cells_y), lambda i: (0, i, 0, 0))]
    return pl.pallas_call(
        gram_kernel if before is None else gram_more_kernel,
        grid=(cells // step,),
        in_specs=in_specs if before is None else in_specs + [whole],
        out_specs=whole,
        out_shape=jax.ShapeDtypeStruct(square, jnp.float32),
        compiler_params=pltpu.CompilerParams(vmem_limit_bytes=20 * MIB),
        name="gram",
    )(*([block] if before is None else [block, before]))


def gram_pack(block, before, place, parts, devices):
    planes_total = before.shape[0]
    group = planes_total // largest_step(planes_total, planes_total // 128)
    rows = len(lower_blocks(planes_total // group)) * group
    rows += -rows % (8 * devices)
    sources, cells, planes, cells_y = block.shape
    step = largest_step(cells, PACK_CELLS)
    vmem = pl.BlockSpec(memory_space=pltpu.VMEM)
    return pl.pallas_call(
        gram_pack_kernel,
        grid=(cells // step,),
        in_specs=[
            pl.BlockSpec(memory_space=pltpu.SMEM),
            pl.BlockSpec((sources, step, planes, cells_y), lambda i: (0, i, 0, 0)),
            vmem,
        ],
        out_specs=[vmem] * parts,
        out_shape=[jax.ShapeDtypeStruct((rows // parts, group), jnp.float32)] * parts,
        scratch_shapes=[pltpu.VMEM(before.shape, jnp.float32)],
        compiler_params=pltpu.CompilerParams(vmem_limit_bytes=20 * MIB),
        name="gram_pack",
    )(place.astype(jnp.int32).reshape(1), block, before)


def inverse_cholesky(matrix):
    size = matrix.shape[0]
    rows = lax.broadcasted_iota(jnp.int32, (size, 2 * size), 0)
    lanes = lax.broadcasted_iota(jnp.int32, (size, size), 1)
    identity = (lanes == rows[:, :size]).astype(jnp.float32)
    work = jnp.concatenate([matrix, identity], axis=1)
    scale = jnp.zeros_like(work)
    for first in range(0, size, PIVOTS):
        columns = [
            jnp.broadcast_to(work[:, first + i : first + i + 1], work.shape) for i in range(PIVOTS)
        ]
        for i in range(PIVOTS):
            j = first + i
            pivot = columns[i][j : j + 1]
            scale = jnp.where(rows == j, lax.rsqrt(pivot), scale)
            factor = jnp.where(rows > j, columns[i] * (1.0 / pivot), 0.0)
            work = work - factor * work[j : j + 1]
            for m in range(i + 1, PIVOTS):
                columns[m] = columns[m] - factor * columns[m][j : j + 1]
    return (work * scale)[:, size:]


def iterate(matrix, subspace):
    for _ in range(ITERS):
        product = nn(subspace, matrix, HIGHEST)
        inverse = inverse_cholesky(nt(product, product, HIGHEST))
        subspace = nn(inverse, product, HIGHEST)
    return subspace


def unpack(place_ref, pieces, packed_ref, gram_ref):
    rows, group = pieces[0].shape
    for n, piece in enumerate(pieces):
        packed_ref[pl.ds(pl.multiple_of(place_ref[n] * rows, 8), rows), :] = piece[...]
    for n, (i, j) in enumerate(lower_blocks(gram_ref.shape[0] // group)):
        block = packed_ref[n * group : (n + 1) * group, :]
        gram_ref[i * group : (i + 1) * group, j * group : (j + 1) * group] = block
        if i != j:
            gram_ref[j * group : (j + 1) * group, i * group : (i + 1) * group] = block.T


def finish_kernel(pieces_count, blocks_count, *refs):
    place_ref, basis_ref = refs[:2]
    pieces = refs[2 : 2 + pieces_count]
    blocks = refs[2 + pieces_count : 2 + pieces_count + blocks_count]
    rest = refs[2 + pieces_count + blocks_count :]
    out_ref, packed_ref, gram_ref, result_ref, in_sems, out_sems = rest[:1] + rest[1:4] + rest[-2:]
    held = rest[4:-2]
    steps, first = [], 0
    for n, block in enumerate(blocks):
        for start in range(0, block.shape[1], PROJECT_CELLS):
            size = min(PROJECT_CELLS, block.shape[1] - start)
            cells = (slice(None), pl.ds(start, size))
            copy = pltpu.make_async_copy(
                block.at[cells], held[n].at[cells], in_sems.at[len(steps)]
            )
            copy.start()
            steps.append((held[n].at[cells], pl.ds(first, size), copy))
            first += size
    unpack(place_ref, pieces, packed_ref, gram_ref)
    subspace = iterate(gram_ref[...], basis_ref[...])
    rank = subspace.shape[0]
    basis_high, basis_low = split(subspace)
    both = jnp.concatenate([basis_high, basis_low], axis=0)
    copies = []
    for n, (block, cells, arrival) in enumerate(steps):
        arrival.wait()
        cells_y = block.shape[3]
        high, low = split(cell_matrix(block))
        main = nn(both, high)
        result = main[:rank] + (main[rank:] + nn(basis_high, low))
        for i in range(cells.size):
            result_ref[cells.start + i] = result[:, i * cells_y : (i + 1) * cells_y]
        copy = pltpu.make_async_copy(result_ref.at[cells], out_ref.at[cells], out_sems.at[n])
        copy.start()
        copies.append(copy)
    for copy in copies:
        copy.wait()


def finish(places, pieces, basis_t, blocks):
    rank, planes_total = basis_t.shape
    cells = sum(block.shape[1] for block in blocks)
    cells_y = blocks[0].shape[3]
    rows, group = pieces[0].shape
    steps = sum(pl.cdiv(block.shape[1], PROJECT_CELLS) for block in blocks)
    vmem = pl.BlockSpec(memory_space=pltpu.VMEM)
    anywhere = pl.BlockSpec(memory_space=pl.ANY)
    out_shape = (cells, rank, cells_y)
    return pl.pallas_call(
        functools.partial(finish_kernel, len(pieces), len(blocks)),
        in_specs=[pl.BlockSpec(memory_space=pltpu.SMEM), vmem]
        + [vmem] * len(pieces)
        + [anywhere] * len(blocks),
        out_specs=anywhere,
        out_shape=jax.ShapeDtypeStruct(out_shape, jnp.float32),
        scratch_shapes=[
            pltpu.VMEM((rows * len(pieces), group), jnp.float32),
            pltpu.VMEM((planes_total, planes_total), jnp.float32),
            pltpu.VMEM(out_shape, jnp.float32),
        ]
        + [pltpu.VMEM(block.shape, jnp.float32) for block in blocks]
        + [pltpu.SemaphoreType.DMA((steps,)), pltpu.SemaphoreType.DMA((steps,))],
        compiler_params=pltpu.CompilerParams(vmem_limit_bytes=32 * MIB),
        name="finish",
    )(places, basis_t, *pieces, *blocks)


def toward(i, step, count):
    return i ^ step if count & (count - 1) == 0 else (i + step) % count


def origin(i, step, count):
    return i ^ step if count & (count - 1) == 0 else (i - step) % count


def inner_size():
    return 2 if lax.axis_size("af") % 2 == 0 else 1


def sum_over_devices(parts):
    groups_af, groups_ta = lax.axis_size("af"), lax.axis_size("ta")
    inner = inner_size()
    outer = groups_af // inner
    me = lax.axis_index("af")
    my_outer, my_inner = me // inner, me % inner

    def to_inner(array):
        return lax.ppermute(array, "af", [(i, i ^ 1) for i in range(groups_af)])

    def to_outer(array, step):
        return lax.ppermute(
            array,
            "af",
            [(i, toward(i // inner, step, outer) * inner + i % inner) for i in range(groups_af)],
        )

    def to_ta(array, step):
        return lax.ppermute(array, "ta", [(i, toward(i, step, groups_ta)) for i in range(groups_ta)])

    def pick(array, index):
        return lax.dynamic_index_in_dim(array, index, 0, False)

    def total(arrays):
        return functools.reduce(jnp.add, arrays)

    mine = parts[0]
    if inner == 2:
        mine = mine + to_inner(parts[1])
    parts = mine.reshape(outer, -1, mine.shape[1])
    mine = total(
        [pick(parts, my_outer)]
        + [to_outer(pick(parts, toward(my_outer, k, outer)), k) for k in range(1, outer)]
    )
    mine = total([mine] + [to_ta(mine, k) for k in range(1, groups_ta)])
    pieces = [mine] + [to_outer(mine, k) for k in range(1, outer)]
    places = [my_inner * outer + origin(my_outer, k, outer) for k in range(outer)]
    if inner == 2:
        pieces += [to_inner(piece) for piece in pieces]
        places += [(1 - my_inner) * outer + origin(my_outer, k, outer) for k in range(outer)]
    return pieces, jnp.stack(places).astype(jnp.int32)


def arrange_kernel(spots, in_ref, out_ref, held_ref, ready_ref, in_sems, out_sems):
    part, targets = held_ref.shape[3], held_ref.shape[2]
    arrivals, sent = [], []
    for n, (frame, x, _, _) in enumerate(spots):
        copy = pltpu.make_async_copy(
            in_ref.at[frame, :, :, pl.ds(x, part)], held_ref.at[n], in_sems.at[n]
        )
        copy.start()
        arrivals.append(copy)
    for n, (_, _, group, cell) in enumerate(spots):
        arrivals[n].wait()
        for target in range(targets):
            ready_ref[n, target] = jnp.swapaxes(held_ref[n, :, target], 0, 1)
        copy = pltpu.make_async_copy(
            ready_ref.at[n],
            out_ref.at[pl.ds(group * targets, targets), pl.ds(cell, part)],
            out_sems.at[n],
        )
        copy.start()
        sent.append(copy)
    for copy in sent:
        copy.wait()


def outgoing(velocity, first, count):
    groups_ta, groups_af = lax.axis_size("ta"), lax.axis_size("af")
    frames, planes, cells_x, cells_y = velocity.shape
    block_frames, block_x = frames // groups_ta, cells_x // groups_af
    part = cell_step(block_x)
    if planes % 8 or part % 8:
        ordered = velocity.reshape(groups_ta, block_frames, planes, groups_af, block_x, cells_y)
        ordered = ordered.transpose(0, 3, 1, 4, 2, 5)
        ordered = ordered.reshape(groups_ta * groups_af, -1, planes, cells_y)
        return ordered[:, first : first + count]
    spots = [
        (group * block_frames + cell // block_x, cell % block_x, group, cell - first)
        for group in range(groups_ta)
        for cell in range(first, first + count, part)
    ]
    anywhere = pl.BlockSpec(memory_space=pl.ANY)
    return pl.pallas_call(
        functools.partial(arrange_kernel, spots),
        in_specs=[anywhere],
        out_specs=anywhere,
        out_shape=pltpu.HBM((groups_ta * groups_af, count, planes, cells_y), jnp.float32),
        scratch_shapes=[
            pltpu.VMEM((len(spots), planes, groups_af, part, cells_y), jnp.float32),
            pltpu.VMEM((len(spots), groups_af, part, planes, cells_y), jnp.float32),
            pltpu.SemaphoreType.DMA((len(spots),)),
            pltpu.SemaphoreType.DMA((len(spots),)),
        ],
        compiler_params=pltpu.CompilerParams(vmem_limit_bytes=56 * MIB),
        name="arrange",
    )(velocity.reshape(frames, planes, groups_af, block_x, cells_y))


def cell_step(block_x):
    return 8 if block_x % 8 == 0 else block_x


def local(velocity, initial_basis):
    groups_ta, groups_af = lax.axis_size("ta"), lax.axis_size("af")
    frames, planes, cells_x, cells_y = velocity.shape
    block_frames, block_x = frames // groups_ta, cells_x // groups_af
    cells, part = block_frames * block_x, cell_step(block_x)
    edge = min(part, cells // 3)
    blocks = []
    for first, count in ((0, edge), (edge, cells - 2 * edge), (cells - edge, edge)):
        block = outgoing(velocity, first, count)
        if blocks:
            block, blocks[-1] = lax.optimization_barrier((block, blocks[-1]))
        block = lax.all_to_all(block, ("ta", "af"), split_axis=0, concat_axis=0, tiled=True)
        blocks.append(block)
    if planes % 8:
        blocks = [
            block.transpose(1, 0, 2, 3).reshape(1, block.shape[1], -1, cells_y) for block in blocks
        ]
    total = gram(blocks[0], None)
    total = gram(blocks[1], total)
    inner = inner_size()
    parts = gram_pack(blocks[2], total, lax.axis_index("af") % inner, inner, groups_af)
    pieces, places = sum_over_devices(parts)
    core = finish(places, pieces, initial_basis.T, blocks)
    return core.reshape(block_frames, block_x, core.shape[1], cells_y)


def solution(mesh):
    placed = (P(None, ("ta", "af"), None, None), P())
    return jax.shard_map(
        local, mesh=mesh, in_specs=placed, out_specs=P("ta", "af", None, None), check_vma=False
    )
```

```python
import functools

import jax
import jax.numpy as jnp
from jax import lax
from jax.experimental import pallas as pl
from jax.experimental.pallas import tpu as pltpu
from jax.sharding import PartitionSpec as P

ITERS = 3
HIGHEST = lax.Precision.HIGHEST
MIB = 1024 * 1024
PIVOTS = 16
PROJECT_CELLS = 8


def split(matrix):
    high = matrix.astype(jnp.bfloat16)
    low = (matrix - high.astype(jnp.float32)).astype(jnp.bfloat16)
    return high, low


def nn(left, right, precision=None):
    return lax.dot_general(
        left, right, (((1,), (0,)), ((), ())), precision=precision,
        preferred_element_type=jnp.float32,
    )


def nt(left, right, precision=None):
    return lax.dot_general(
        left, right, (((1,), (1,)), ((), ())), precision=precision,
        preferred_element_type=jnp.float32,
    )


def largest_step(extent, most):
    step = min(extent, most)
    while extent % step:
        step -= 1
    return step


def cell_matrix(block_ref):
    sources, cells, planes, cells_y = block_ref.shape
    return jnp.concatenate(
        [block_ref[:, i].reshape(sources * planes, cells_y) for i in range(cells)], axis=1
    )


def lower_segments(count):
    below = [(i, j, half) for i in range(count) for j in range(i) for half in range(2)]
    return below + [(i, i, 1) for i in range(count)] + [(i, i, 0) for i in range(0, count, 2)]


def piece_sizes(cells):
    sizes, size = [], 4
    while cells:
        sizes.append(min(size, cells))
        cells -= sizes[-1]
        size = min(3 * size, 24)
    return sizes


def gram_pack_kernel(block_ref, *refs):
    parts, held_ref, total_ref, sems = refs[:-3], refs[-3], refs[-2], refs[-1]
    arrivals, first = [], 0
    for n, size in enumerate(piece_sizes(block_ref.shape[1])):
        view = (slice(None), pl.ds(first, size))
        copy = pltpu.make_async_copy(block_ref.at[view], held_ref.at[view], sems.at[n])
        copy.start()
        arrivals.append((copy, view))
        first += size
    rows, group = parts[0].shape
    planes_total = total_ref.shape[0]
    half = planes_total // 2 // group * group
    for n, (copy, view) in enumerate(arrivals):
        copy.wait()
        high, low = split(cell_matrix(held_ref.at[view]))
        mixed = nt(high, low * jnp.bfloat16(2))
        total_ref[...] = mixed if n == 0 else total_ref[...] + mixed
        total_ref[:half, :half] += nt(high[:half], high[:half])
        doubled = jnp.concatenate([high[:half] * jnp.bfloat16(2), high[half:]], axis=0)
        total_ref[half:, :] += nt(high[half:], doubled)
    for i in range(planes_total // group):
        for j in range(i + 1):
            here = pl.ds(i * group, group), pl.ds(j * group, group)
            there = pl.ds(j * group, group), pl.ds(i * group, group)
            total_ref[here] = 0.5 * (total_ref[here] + total_ref[there].T)
    my_inner = lax.rem(lax.axis_index("af"), len(parts))
    for place in range(len(parts)):

        @pl.when(my_inner == place)
        def _(place=place):
            for k, part_ref in enumerate(parts):
                start = (place + k) % len(parts) * rows
                copy_rows(part_ref, start, total_ref)


def copy_rows(part_ref, start, total_ref):
    group = part_ref.shape[1]
    half = group // 2
    segments = lower_segments(total_ref.shape[0] // group)

    def quarter(i, skip, size):
        first = i * group
        if first >= total_ref.shape[0]:
            return jnp.zeros((size, half), jnp.float32)
        return total_ref[first + skip : first + skip + size, first : first + half]

    done = 0
    while done < part_ref.shape[0]:
        n, skip = divmod(start + done, half)
        size = min(half - skip, part_ref.shape[0] - done)
        if n >= len(segments):
            value = jnp.zeros((size, group), jnp.float32)
        else:
            i, j, lower = segments[n]
            if i == j and not lower:
                value = jnp.concatenate([quarter(i, skip, size), quarter(i + 1, skip, size)], axis=1)
            else:
                first = i * group + lower * half + skip
                value = total_ref[first : first + size, j * group : (j + 1) * group]
        part_ref[done : done + size, :] = value
        done += size


def gram_pack(block, parts, devices):
    planes_total = block.shape[0] * block.shape[2]
    group = planes_total // largest_step(planes_total, planes_total // 128)
    rows = len(lower_segments(planes_total // group)) * (group // 2)
    rows += -rows % (8 * devices)
    vmem = pl.BlockSpec(memory_space=pltpu.VMEM)
    return pl.pallas_call(
        gram_pack_kernel,
        in_specs=[pl.BlockSpec(memory_space=pl.ANY)],
        out_specs=[vmem] * parts,
        out_shape=[jax.ShapeDtypeStruct((rows // parts, group), jnp.float32)] * parts,
        scratch_shapes=[
            pltpu.VMEM(block.shape, jnp.float32),
            pltpu.VMEM((planes_total, planes_total), jnp.float32),
            pltpu.SemaphoreType.DMA((len(piece_sizes(block.shape[1])),)),
        ],
        compiler_params=pltpu.CompilerParams(vmem_limit_bytes=48 * MIB),
        name="gram_pack",
    )(block)


def inverse_cholesky(matrix):
    size = matrix.shape[0]
    step = largest_step(size, PIVOTS)
    ones = lax.broadcasted_iota(jnp.int32, (size, size), 0) == lax.broadcasted_iota(
        jnp.int32, (size, size), 1
    )
    work = jnp.concatenate([matrix, ones.astype(jnp.float32)], axis=1)
    work = [work[first : first + step] for first in range(0, size, step)]
    shape = work[0].shape
    rows = lax.broadcasted_iota(jnp.int32, shape, 0)
    done = []
    for n in range(len(work)):
        scale = jnp.zeros(shape, jnp.float32)
        columns = {
            m: [
                jnp.broadcast_to(work[m][:, lane : lane + 1], shape)
                for lane in range(n * step, (n + 1) * step)
            ]
            for m in range(n, len(work))
        }
        for i in range(step):
            pivot = columns[n][i][i : i + 1]
            scale = jnp.where(rows == i, lax.rsqrt(pivot), scale)
            inverse = 1.0 / pivot
            row = work[n][i : i + 1] * inverse
            others = [columns[n][k][i : i + 1] * inverse for k in range(i + 1, step)]
            for m in range(n, len(work)):
                factor = columns[m][i]
                if m == n:
                    factor = jnp.where(rows > i, factor, 0.0)
                work[m] = work[m] - factor * row
                for k, other in enumerate(others):
                    columns[m][i + 1 + k] = columns[m][i + 1 + k] - factor * other
        done.append(work[n] * scale)
    return jnp.concatenate(done, axis=0)[:, size:]


def split_three(matrix):
    high, low = split(matrix)
    rest = matrix - high.astype(jnp.float32) - low.astype(jnp.float32)
    return high, low, rest.astype(jnp.bfloat16)


def iterate(matrix, subspace):
    matrix_high, matrix_low, matrix_rest = split_three(matrix)
    rank = subspace.shape[0]
    for _ in range(ITERS):
        high, low, rest = split_three(subspace)
        by_high = nn(jnp.concatenate([high, low, rest], axis=0), matrix_high)
        by_low = nn(jnp.concatenate([high, low], axis=0), matrix_low)
        small = by_high[2 * rank :] + by_low[rank:] + nn(high, matrix_rest)
        product = by_high[:rank] + (by_high[rank : 2 * rank] + by_low[:rank] + small)
        inverse = inverse_cholesky(nt(product, product, HIGHEST))
        subspace = nn(inverse, product, HIGHEST)
    return subspace


def unpack(places, pieces, packed_ref, gram_ref):
    rows, group = pieces[0].shape
    for n, piece in enumerate(pieces):
        packed_ref[pl.ds(pl.multiple_of(places[n] * rows, 8), rows), :] = piece[...]
    half = group // 2
    for n, (i, j, lower) in enumerate(lower_segments(gram_ref.shape[0] // group)):
        segment = packed_ref[n * half : (n + 1) * half, :]
        rows_here = pl.ds(i * group + lower * half, half)
        if i != j:
            gram_ref[rows_here, j * group : (j + 1) * group] = segment
            mirrored = pl.ds(i * group + lower * half, half)
            gram_ref[j * group : (j + 1) * group, mirrored] = segment.T
        elif lower:
            gram_ref[rows_here, i * group : (i + 1) * group] = segment
            gram_ref[i * group : i * group + half, i * group + half : (i + 1) * group] = (
                segment[:, :half].T
            )
        else:
            for k in range(2):
                first = (i + k) * group
                if first < gram_ref.shape[0]:
                    gram_ref[first : first + half, first : first + half] = (
                        segment[:, k * half : (k + 1) * half]
                    )


def finish_kernel(pieces_count, blocks_count, *refs):
    basis_ref = refs[0]
    pieces = refs[1 : 1 + pieces_count]
    blocks = refs[1 + pieces_count : 1 + pieces_count + blocks_count]
    rest = refs[1 + pieces_count + blocks_count :]
    out_ref, packed_ref, gram_ref, result_ref, in_sems, out_sems = rest[:1] + rest[1:4] + rest[-2:]
    held = rest[4:-2]
    steps, first = [], 0
    for n, block in enumerate(blocks):
        for start in range(0, block.shape[1], PROJECT_CELLS):
            size = min(PROJECT_CELLS, block.shape[1] - start)
            cells = (slice(None), pl.ds(start, size))
            copy = pltpu.make_async_copy(
                block.at[cells], held[n].at[cells], in_sems.at[len(steps)]
            )
            copy.start()
            steps.append((held[n].at[cells], pl.ds(first, size), copy))
            first += size
    unpack(piece_places(), pieces, packed_ref, gram_ref)
    subspace = iterate(gram_ref[...], basis_ref[...])
    rank = subspace.shape[0]
    basis_high, basis_low = split(subspace)
    both = jnp.concatenate([basis_high, basis_low], axis=0)
    copies = []
    for n, (block, cells, arrival) in enumerate(steps):
        arrival.wait()
        cells_y = block.shape[3]
        high, low = split(cell_matrix(block))
        main = nn(both, high)
        result = main[:rank] + (main[rank:] + nn(basis_high, low))
        for i in range(cells.size):
            result_ref[cells.start + i] = result[:, i * cells_y : (i + 1) * cells_y]
        copy = pltpu.make_async_copy(result_ref.at[cells], out_ref.at[cells], out_sems.at[n])
        copy.start()
        copies.append(copy)
    for copy in copies:
        copy.wait()


def finish(pieces, basis_t, blocks):
    rank, planes_total = basis_t.shape
    cells = sum(block.shape[1] for block in blocks)
    cells_y = blocks[0].shape[3]
    rows, group = pieces[0].shape
    steps = sum(pl.cdiv(block.shape[1], PROJECT_CELLS) for block in blocks)
    vmem = pl.BlockSpec(memory_space=pltpu.VMEM)
    anywhere = pl.BlockSpec(memory_space=pl.ANY)
    out_shape = (cells, rank, cells_y)
    return pl.pallas_call(
        functools.partial(finish_kernel, len(pieces), len(blocks)),
        in_specs=[vmem] * (1 + len(pieces))
        + [anywhere] * len(blocks),
        out_specs=anywhere,
        out_shape=jax.ShapeDtypeStruct(out_shape, jnp.float32),
        scratch_shapes=[
            pltpu.VMEM((rows * len(pieces), group), jnp.float32),
            pltpu.VMEM((planes_total, planes_total), jnp.float32),
            pltpu.VMEM(out_shape, jnp.float32),
        ]
        + [pltpu.VMEM(block.shape, jnp.float32) for block in blocks]
        + [pltpu.SemaphoreType.DMA((steps,)), pltpu.SemaphoreType.DMA((steps,))],
        compiler_params=pltpu.CompilerParams(vmem_limit_bytes=56 * MIB),
        name="finish",
    )(basis_t, *pieces, *blocks)


def toward(i, step, count):
    return i ^ step if count & (count - 1) == 0 else (i + step) % count


def origin(i, step, count):
    return i ^ step if count & (count - 1) == 0 else (i - step) % count


def inner_size():
    return 2 if lax.axis_size("af") % 2 == 0 else 1


def af_place():
    inner = inner_size()
    me = lax.axis_index("af")
    return lax.div(me, inner), lax.rem(me, inner), lax.axis_size("af") // inner


def piece_places():
    my_outer, my_inner, outer = af_place()
    places = []
    for i in range(inner_size()):
        group = my_inner if i == 0 else 1 - my_inner
        places += [group * outer + origin(my_outer, k, outer) for k in range(outer)]
    return places


def cut_kernel(kept_ref, came_ref, *refs):
    outs, total_ref = refs[:-1], refs[-1]
    my_outer, _, outer = af_place()
    total_ref[...] = kept_ref[...] + came_ref[...]
    rows = outs[0].shape[0]
    for k, out_ref in enumerate(outs):
        start = toward(my_outer, k, outer) * rows
        out_ref[...] = total_ref[pl.ds(pl.multiple_of(start, 8), rows), :]


def cut(kept, came, outer):
    rows, group = kept.shape
    vmem = pl.BlockSpec(memory_space=pltpu.VMEM)
    return pl.pallas_call(
        cut_kernel,
        in_specs=[vmem] * 2,
        out_specs=[vmem] * outer,
        out_shape=[jax.ShapeDtypeStruct((rows // outer, group), jnp.float32)] * outer,
        scratch_shapes=[pltpu.VMEM(kept.shape, jnp.float32)],
        compiler_params=pltpu.CompilerParams(vmem_limit_bytes=8 * MIB),
        name="cut",
    )(kept, came)


def sum_over_devices(parts):
    groups_af, groups_ta = lax.axis_size("af"), lax.axis_size("ta")
    inner = inner_size()
    outer = groups_af // inner

    def to_inner(array):
        return lax.ppermute(array, "af", [(i, i ^ 1) for i in range(groups_af)])

    def to_outer(array, step):
        return lax.ppermute(
            array,
            "af",
            [(i, toward(i // inner, step, outer) * inner + i % inner) for i in range(groups_af)],
        )

    def to_ta(array, step):
        return lax.ppermute(array, "ta", [(i, toward(i, step, groups_ta)) for i in range(groups_ta)])

    def total(arrays):
        return functools.reduce(jnp.add, arrays)

    came = to_inner(parts[1]) if inner == 2 else jnp.zeros_like(parts[0])
    parts = cut(parts[0], came, outer)
    mine = total([parts[0]] + [to_outer(parts[k], k) for k in range(1, outer)])
    mine = total([mine] + [to_ta(mine, k) for k in range(1, groups_ta)])
    pieces = [mine] + [to_outer(mine, k) for k in range(1, outer)]
    if inner == 2:
        pieces += [to_inner(piece) for piece in pieces]
    return pieces


def arrange_kernel(spots, in_ref, out_ref, held_ref, ready_ref, in_sems, out_sems):
    part, targets = held_ref.shape[3], held_ref.shape[2]
    arrivals, sent = [], []
    for n, (frame, x, _, _) in enumerate(spots):
        copy = pltpu.make_async_copy(
            in_ref.at[frame, :, :, pl.ds(x, part)], held_ref.at[n], in_sems.at[n]
        )
        copy.start()
        arrivals.append(copy)
    for n, (_, _, group, cell) in enumerate(spots):
        arrivals[n].wait()
        for target in range(targets):
            ready_ref[n, target] = jnp.swapaxes(held_ref[n, :, target], 0, 1)
        copy = pltpu.make_async_copy(
            ready_ref.at[n],
            out_ref.at[pl.ds(group * targets, targets), pl.ds(cell, part)],
            out_sems.at[n],
        )
        copy.start()
        sent.append(copy)
    for copy in sent:
        copy.wait()


def outgoing(velocity):
    groups_ta, groups_af = lax.axis_size("ta"), lax.axis_size("af")
    frames, planes, cells_x, cells_y = velocity.shape
    block_frames, block_x = frames // groups_ta, cells_x // groups_af
    cells = block_frames * block_x
    if planes % 8 or block_x % 8:
        ordered = velocity.reshape(groups_ta, block_frames, planes, groups_af, block_x, cells_y)
        ordered = ordered.transpose(0, 3, 1, 4, 2, 5)
        return ordered.reshape(groups_ta * groups_af, cells, planes, cells_y)
    spots = [
        (group * block_frames + frame, 0, group, frame * block_x)
        for group in range(groups_ta)
        for frame in range(block_frames)
    ]
    anywhere = pl.BlockSpec(memory_space=pl.ANY)
    return pl.pallas_call(
        functools.partial(arrange_kernel, spots),
        in_specs=[anywhere],
        out_specs=anywhere,
        out_shape=pltpu.HBM((groups_ta * groups_af, cells, planes, cells_y), jnp.float32),
        scratch_shapes=[
            pltpu.VMEM((len(spots), planes, groups_af, block_x, cells_y), jnp.float32),
            pltpu.VMEM((len(spots), groups_af, block_x, planes, cells_y), jnp.float32),
            pltpu.SemaphoreType.DMA((len(spots),)),
            pltpu.SemaphoreType.DMA((len(spots),)),
        ],
        compiler_params=pltpu.CompilerParams(vmem_limit_bytes=56 * MIB),
        name="arrange",
    )(velocity.reshape(frames, planes, groups_af, block_x, cells_y))


def local(velocity, initial_basis):
    groups_ta, groups_af = lax.axis_size("ta"), lax.axis_size("af")
    frames, planes, cells_x, cells_y = velocity.shape
    block_frames, block_x = frames // groups_ta, cells_x // groups_af
    block = lax.all_to_all(
        outgoing(velocity), ("ta", "af"), split_axis=0, concat_axis=0, tiled=True
    )
    if planes % 8:
        block = block.transpose(1, 0, 2, 3).reshape(1, block.shape[1], -1, cells_y)
    inner = inner_size()
    pieces = sum_over_devices(gram_pack(block, inner, groups_af))
    core = finish(pieces, initial_basis.T, [block])
    return core.reshape(block_frames, block_x, core.shape[1], cells_y)


def solution(mesh):
    placed = (P(None, ("ta", "af"), None, None), P())
    return jax.shard_map(
        local, mesh=mesh, in_specs=placed, out_specs=P("ta", "af", None, None), check_vma=False
    )
```

```python
import functools

import jax
import jax.numpy as jnp
from jax import lax
from jax.experimental import pallas as pl
from jax.experimental.pallas import tpu as pltpu
from jax.sharding import PartitionSpec as P

ITERS = 3
HIGHEST = lax.Precision.HIGHEST
MIB = 1024 * 1024
PIVOTS = 16
PROJECT_CELLS = 8


def split(matrix):
    high = matrix.astype(jnp.bfloat16)
    low = (matrix - high.astype(jnp.float32)).astype(jnp.bfloat16)
    return high, low


def nn(left, right, precision=None):
    return lax.dot_general(
        left, right, (((1,), (0,)), ((), ())), precision=precision,
        preferred_element_type=jnp.float32,
    )


def nt(left, right, precision=None):
    return lax.dot_general(
        left, right, (((1,), (1,)), ((), ())), precision=precision,
        preferred_element_type=jnp.float32,
    )


def largest_step(extent, most):
    step = min(extent, most)
    while extent % step:
        step -= 1
    return step


def cell_matrix(block_ref):
    sources, cells, planes, cells_y = block_ref.shape
    return jnp.concatenate(
        [block_ref[:, i].reshape(sources * planes, cells_y) for i in range(cells)], axis=1
    )


def lower_segments(count):
    below = [(i, j, half) for i in range(count) for j in range(i) for half in range(2)]
    return below + [(i, i, 1) for i in range(count)] + [(i, i, 0) for i in range(0, count, 2)]


def piece_sizes(cells):
    sizes, size = [], 4
    while cells:
        sizes.append(min(size, cells))
        cells -= sizes[-1]
        size = min(3 * size, 24)
    return sizes


def gram_pack_kernel(block_ref, *refs):
    parts, held_ref, total_ref, sems = refs[:-3], refs[-3], refs[-2], refs[-1]
    arrivals, first = [], 0
    for n, size in enumerate(piece_sizes(block_ref.shape[1])):
        view = (slice(None), pl.ds(first, size))
        copy = pltpu.make_async_copy(block_ref.at[view], held_ref.at[view], sems.at[n])
        copy.start()
        arrivals.append((copy, view))
        first += size
    rows, group = parts[0].shape
    planes_total = total_ref.shape[0]
    half = planes_total // 2 // group * group
    for n, (copy, view) in enumerate(arrivals):
        copy.wait()
        high, low = split(cell_matrix(held_ref.at[view]))
        mixed = nt(high, low * jnp.bfloat16(2))
        total_ref[...] = mixed if n == 0 else total_ref[...] + mixed
        total_ref[:half, :half] += nt(high[:half], high[:half])
        doubled = jnp.concatenate([high[:half] * jnp.bfloat16(2), high[half:]], axis=0)
        total_ref[half:, :] += nt(high[half:], doubled)
    for i in range(planes_total // group):
        for j in range(i + 1):
            here = pl.ds(i * group, group), pl.ds(j * group, group)
            there = pl.ds(j * group, group), pl.ds(i * group, group)
            total_ref[here] = 0.5 * (total_ref[here] + total_ref[there].T)
    my_inner = lax.rem(lax.axis_index("af"), len(parts))
    for place in range(len(parts)):

        @pl.when(my_inner == place)
        def _(place=place):
            for k, part_ref in enumerate(parts):
                start = (place + k) % len(parts) * rows
                copy_rows(part_ref, start, total_ref)


def copy_rows(part_ref, start, total_ref):
    group = part_ref.shape[1]
    half = group // 2
    segments = lower_segments(total_ref.shape[0] // group)

    def quarter(i, skip, size):
        first = i * group
        if first >= total_ref.shape[0]:
            return jnp.zeros((size, half), jnp.float32)
        return total_ref[first + skip : first + skip + size, first : first + half]

    done = 0
    while done < part_ref.shape[0]:
        n, skip = divmod(start + done, half)
        size = min(half - skip, part_ref.shape[0] - done)
        if n >= len(segments):
            value = jnp.zeros((size, group), jnp.float32)
        else:
            i, j, lower = segments[n]
            if i == j and not lower:
                value = jnp.concatenate([quarter(i, skip, size), quarter(i + 1, skip, size)], axis=1)
            else:
                first = i * group + lower * half + skip
                value = total_ref[first : first + size, j * group : (j + 1) * group]
        part_ref[done : done + size, :] = value
        done += size


def gram_pack(block, parts, devices):
    planes_total = block.shape[0] * block.shape[2]
    group = planes_total // largest_step(planes_total, planes_total // 128)
    rows = len(lower_segments(planes_total // group)) * (group // 2)
    rows += -rows % (8 * devices)
    vmem = pl.BlockSpec(memory_space=pltpu.VMEM)
    return pl.pallas_call(
        gram_pack_kernel,
        in_specs=[pl.BlockSpec(memory_space=pl.ANY)],
        out_specs=[vmem] * parts,
        out_shape=[jax.ShapeDtypeStruct((rows // parts, group), jnp.float32)] * parts,
        scratch_shapes=[
            pltpu.VMEM(block.shape, jnp.float32),
            pltpu.VMEM((planes_total, planes_total), jnp.float32),
            pltpu.SemaphoreType.DMA((len(piece_sizes(block.shape[1])),)),
        ],
        compiler_params=pltpu.CompilerParams(vmem_limit_bytes=48 * MIB),
        name="gram_pack",
    )(block)


def inverse_cholesky(matrix):
    size = matrix.shape[0]
    step = largest_step(size, PIVOTS)
    ones = lax.broadcasted_iota(jnp.int32, (size, size), 0) == lax.broadcasted_iota(
        jnp.int32, (size, size), 1
    )
    work = jnp.concatenate([matrix, ones.astype(jnp.float32)], axis=1)
    work = [work[first : first + step] for first in range(0, size, step)]
    shape = work[0].shape
    rows = lax.broadcasted_iota(jnp.int32, shape, 0)
    done = []
    for n in range(len(work)):
        scale = jnp.zeros(shape, jnp.float32)
        columns = {
            m: [
                jnp.broadcast_to(work[m][:, lane : lane + 1], shape)
                for lane in range(n * step, (n + 1) * step)
            ]
            for m in range(n, len(work))
        }
        for i in range(step):
            pivot = columns[n][i][i : i + 1]
            scale = jnp.where(rows == i, lax.rsqrt(pivot), scale)
            inverse = 1.0 / pivot
            row = work[n][i : i + 1] * inverse
            others = [columns[n][k][i : i + 1] * inverse for k in range(i + 1, step)]
            for m in range(n, len(work)):
                factor = columns[m][i]
                if m == n:
                    factor = jnp.where(rows > i, factor, 0.0)
                work[m] = work[m] - factor * row
                for k, other in enumerate(others):
                    columns[m][i + 1 + k] = columns[m][i + 1 + k] - factor * other
        done.append(work[n] * scale)
    return jnp.concatenate(done, axis=0)[:, size:]


def split_three(matrix):
    high, low = split(matrix)
    rest = matrix - high.astype(jnp.float32) - low.astype(jnp.float32)
    return high, low, rest.astype(jnp.bfloat16)


def iterate(matrix, subspace):
    matrix_high, matrix_low, matrix_rest = split_three(matrix)
    rank = subspace.shape[0]
    for _ in range(ITERS):
        high, low, rest = split_three(subspace)
        by_high = nn(jnp.concatenate([high, low, rest], axis=0), matrix_high)
        by_low = nn(jnp.concatenate([high, low], axis=0), matrix_low)
        small = by_high[2 * rank :] + by_low[rank:] + nn(high, matrix_rest)
        product = by_high[:rank] + (by_high[rank : 2 * rank] + by_low[:rank] + small)
        inverse = inverse_cholesky(nt(product, product, HIGHEST))
        subspace = nn(inverse, product, HIGHEST)
    return subspace


def unpack(places, pieces, packed_ref, gram_ref):
    rows, group = pieces[0].shape
    for n, piece in enumerate(pieces):
        packed_ref[pl.ds(pl.multiple_of(places[n] * rows, 8), rows), :] = piece[...]
    half = group // 2
    for n, (i, j, lower) in enumerate(lower_segments(gram_ref.shape[0] // group)):
        segment = packed_ref[n * half : (n + 1) * half, :]
        rows_here = pl.ds(i * group + lower * half, half)
        if i != j:
            gram_ref[rows_here, j * group : (j + 1) * group] = segment
            mirrored = pl.ds(i * group + lower * half, half)
            gram_ref[j * group : (j + 1) * group, mirrored] = segment.T
        elif lower:
            gram_ref[rows_here, i * group : (i + 1) * group] = segment
            gram_ref[i * group : i * group + half, i * group + half : (i + 1) * group] = (
                segment[:, :half].T
            )
        else:
            for k in range(2):
                first = (i + k) * group
                if first < gram_ref.shape[0]:
                    gram_ref[first : first + half, first : first + half] = (
                        segment[:, k * half : (k + 1) * half]
                    )


def finish_kernel(pieces_count, blocks_count, *refs):
    basis_ref = refs[0]
    pieces = refs[1 : 1 + pieces_count]
    blocks = refs[1 + pieces_count : 1 + pieces_count + blocks_count]
    rest = refs[1 + pieces_count + blocks_count :]
    out_ref, packed_ref, gram_ref, result_ref, in_sems, out_sems = rest[:1] + rest[1:4] + rest[-2:]
    held = rest[4:-2]
    steps, first = [], 0
    for n, block in enumerate(blocks):
        for start in range(0, block.shape[1], PROJECT_CELLS):
            size = min(PROJECT_CELLS, block.shape[1] - start)
            cells = (slice(None), pl.ds(start, size))
            copy = pltpu.make_async_copy(
                block.at[cells], held[n].at[cells], in_sems.at[len(steps)]
            )
            copy.start()
            steps.append((held[n].at[cells], pl.ds(first, size), copy))
            first += size
    unpack(piece_places(), pieces, packed_ref, gram_ref)
    subspace = iterate(gram_ref[...], basis_ref[...])
    rank = subspace.shape[0]
    basis_high, basis_low = split(subspace)
    both = jnp.concatenate([basis_high, basis_low], axis=0)
    copies = []
    for n, (block, cells, arrival) in enumerate(steps):
        arrival.wait()
        cells_y = block.shape[3]
        high, low = split(cell_matrix(block))
        main = nn(both, high)
        result = main[:rank] + (main[rank:] + nn(basis_high, low))
        for i in range(cells.size):
            result_ref[cells.start + i] = result[:, i * cells_y : (i + 1) * cells_y]
        copy = pltpu.make_async_copy(result_ref.at[cells], out_ref.at[cells], out_sems.at[n])
        copy.start()
        copies.append(copy)
    for copy in copies:
        copy.wait()


def finish(pieces, basis_t, blocks):
    rank, planes_total = basis_t.shape
    cells = sum(block.shape[1] for block in blocks)
    cells_y = blocks[0].shape[3]
    rows, group = pieces[0].shape
    steps = sum(pl.cdiv(block.shape[1], PROJECT_CELLS) for block in blocks)
    vmem = pl.BlockSpec(memory_space=pltpu.VMEM)
    anywhere = pl.BlockSpec(memory_space=pl.ANY)
    out_shape = (cells, rank, cells_y)
    return pl.pallas_call(
        functools.partial(finish_kernel, len(pieces), len(blocks)),
        in_specs=[vmem] * (1 + len(pieces))
        + [anywhere] * len(blocks),
        out_specs=anywhere,
        out_shape=jax.ShapeDtypeStruct(out_shape, jnp.float32),
        scratch_shapes=[
            pltpu.VMEM((rows * len(pieces), group), jnp.float32),
            pltpu.VMEM((planes_total, planes_total), jnp.float32),
            pltpu.VMEM(out_shape, jnp.float32),
        ]
        + [pltpu.VMEM(block.shape, jnp.float32) for block in blocks]
        + [pltpu.SemaphoreType.DMA((steps,)), pltpu.SemaphoreType.DMA((steps,))],
        compiler_params=pltpu.CompilerParams(vmem_limit_bytes=56 * MIB),
        name="finish",
    )(basis_t, *pieces, *blocks)


def toward(i, step, count):
    return i ^ step if count & (count - 1) == 0 else (i + step) % count


def origin(i, step, count):
    return i ^ step if count & (count - 1) == 0 else (i - step) % count


def inner_size():
    return 2 if lax.axis_size("af") % 2 == 0 else 1


def af_place():
    inner = inner_size()
    me = lax.axis_index("af")
    return lax.div(me, inner), lax.rem(me, inner), lax.axis_size("af") // inner


def piece_places():
    my_outer, my_inner, outer = af_place()
    places = []
    for i in range(inner_size()):
        group = my_inner if i == 0 else 1 - my_inner
        places += [group * outer + origin(my_outer, k, outer) for k in range(outer)]
    return places


def cut_kernel(kept_ref, came_ref, *refs):
    outs, total_ref = refs[:-1], refs[-1]
    my_outer, _, outer = af_place()
    total_ref[...] = kept_ref[...] + came_ref[...]
    rows = outs[0].shape[0]
    for k, out_ref in enumerate(outs):
        start = toward(my_outer, k, outer) * rows
        out_ref[...] = total_ref[pl.ds(pl.multiple_of(start, 8), rows), :]


def cut(kept, came, outer):
    rows, group = kept.shape
    vmem = pl.BlockSpec(memory_space=pltpu.VMEM)
    return pl.pallas_call(
        cut_kernel,
        in_specs=[vmem] * 2,
        out_specs=[vmem] * outer,
        out_shape=[jax.ShapeDtypeStruct((rows // outer, group), jnp.float32)] * outer,
        scratch_shapes=[pltpu.VMEM(kept.shape, jnp.float32)],
        compiler_params=pltpu.CompilerParams(vmem_limit_bytes=8 * MIB),
        name="cut",
    )(kept, came)


def sum_over_devices(parts):
    groups_af, groups_ta = lax.axis_size("af"), lax.axis_size("ta")
    inner = inner_size()
    outer = groups_af // inner

    def to_inner(array):
        return lax.ppermute(array, "af", [(i, i ^ 1) for i in range(groups_af)])

    def to_outer(array, step):
        return lax.ppermute(
            array,
            "af",
            [(i, toward(i // inner, step, outer) * inner + i % inner) for i in range(groups_af)],
        )

    def to_ta(array, step):
        return lax.ppermute(array, "ta", [(i, toward(i, step, groups_ta)) for i in range(groups_ta)])

    def total(arrays):
        return functools.reduce(jnp.add, arrays)

    came = to_inner(parts[1]) if inner == 2 else jnp.zeros_like(parts[0])
    parts = cut(parts[0], came, outer)
    mine = total([parts[0]] + [to_outer(parts[k], k) for k in range(1, outer)])
    mine = total([mine] + [to_ta(mine, k) for k in range(1, groups_ta)])
    pieces = [mine] + [to_outer(mine, k) for k in range(1, outer)]
    if inner == 2:
        pieces += [to_inner(piece) for piece in pieces]
    return pieces


def arrange_kernel(spots, in_ref, out_ref, held_ref, sems):
    part, targets = held_ref.shape[3], held_ref.shape[2]
    arrivals = []
    for n, (frame, x, _, _) in enumerate(spots):
        copy = pltpu.make_async_copy(
            in_ref.at[frame, :, :, pl.ds(x, part)], held_ref.at[n], sems.at[n]
        )
        copy.start()
        arrivals.append(copy)
    for n, (_, _, group, cell) in enumerate(spots):
        arrivals[n].wait()
        for target in range(targets):
            out_ref[group * targets + target, cell : cell + part] = jnp.swapaxes(
                held_ref[n, :, target], 0, 1
            )


def outgoing(velocity):
    groups_ta, groups_af = lax.axis_size("ta"), lax.axis_size("af")
    frames, planes, cells_x, cells_y = velocity.shape
    block_frames, block_x = frames // groups_ta, cells_x // groups_af
    cells = block_frames * block_x
    if planes % 8 or block_x % 8:
        ordered = velocity.reshape(groups_ta, block_frames, planes, groups_af, block_x, cells_y)
        ordered = ordered.transpose(0, 3, 1, 4, 2, 5)
        return ordered.reshape(groups_ta * groups_af, cells, planes, cells_y)
    spots = [
        (group * block_frames + frame, 0, group, frame * block_x)
        for group in range(groups_ta)
        for frame in range(block_frames)
    ]
    anywhere = pl.BlockSpec(memory_space=pl.ANY)
    return pl.pallas_call(
        functools.partial(arrange_kernel, spots),
        in_specs=[anywhere],
        out_specs=pl.BlockSpec(memory_space=pltpu.VMEM),
        out_shape=jax.ShapeDtypeStruct(
            (groups_ta * groups_af, cells, planes, cells_y), jnp.float32
        ),
        scratch_shapes=[
            pltpu.VMEM((len(spots), planes, groups_af, block_x, cells_y), jnp.float32),
            pltpu.SemaphoreType.DMA((len(spots),)),
        ],
        compiler_params=pltpu.CompilerParams(vmem_limit_bytes=30 * MIB),
        name="arrange",
    )(velocity.reshape(frames, planes, groups_af, block_x, cells_y))


def local(velocity, initial_basis):
    groups_ta, groups_af = lax.axis_size("ta"), lax.axis_size("af")
    frames, planes, cells_x, cells_y = velocity.shape
    block_frames, block_x = frames // groups_ta, cells_x // groups_af
    block = lax.all_to_all(
        outgoing(velocity), ("ta", "af"), split_axis=0, concat_axis=0, tiled=True
    )
    if planes % 8:
        block = block.transpose(1, 0, 2, 3).reshape(1, block.shape[1], -1, cells_y)
    inner = inner_size()
    pieces = sum_over_devices(gram_pack(block, inner, groups_af))
    core = finish(pieces, initial_basis.T, [block])
    return core.reshape(block_frames, block_x, core.shape[1], cells_y)


def solution(mesh):
    placed = (P(None, ("ta", "af"), None, None), P())
    return jax.shard_map(
        local, mesh=mesh, in_specs=placed, out_specs=P("ta", "af", None, None), check_vma=False
    )
```

```python
import functools

import jax
import jax.numpy as jnp
from jax import lax
from jax.experimental import pallas as pl
from jax.experimental.pallas import tpu as pltpu
from jax.sharding import PartitionSpec as P

ITERS = 3
HIGHEST = lax.Precision.HIGHEST
MIB = 1024 * 1024
PIVOTS = 16
PROJECT_CELLS = 8


def split(matrix):
    high = matrix.astype(jnp.bfloat16)
    low = (matrix - high.astype(jnp.float32)).astype(jnp.bfloat16)
    return high, low


def nn(left, right, precision=None):
    return lax.dot_general(
        left, right, (((1,), (0,)), ((), ())), precision=precision,
        preferred_element_type=jnp.float32,
    )


def nt(left, right, precision=None):
    return lax.dot_general(
        left, right, (((1,), (1,)), ((), ())), precision=precision,
        preferred_element_type=jnp.float32,
    )


def largest_step(extent, most):
    step = min(extent, most)
    while extent % step:
        step -= 1
    return step


def cell_matrix(block_ref):
    sources, cells, planes, cells_y = block_ref.shape
    return jnp.concatenate(
        [block_ref[:, i].reshape(sources * planes, cells_y) for i in range(cells)], axis=1
    )


def lower_segments(count):
    below = [(i, j, half) for i in range(count) for j in range(i) for half in range(2)]
    return below + [(i, i, 1) for i in range(count)] + [(i, i, 0) for i in range(0, count, 2)]


def piece_sizes(cells):
    sizes, size = [], 4
    while cells:
        sizes.append(min(size, cells))
        cells -= sizes[-1]
        size = min(3 * size, 24)
    return sizes


def gram_pack_kernel(block_ref, *refs):
    parts, held_ref, total_ref, sems = refs[:-3], refs[-3], refs[-2], refs[-1]
    arrivals, first = [], 0
    for n, size in enumerate(piece_sizes(block_ref.shape[1])):
        view = (slice(None), pl.ds(first, size))
        copy = pltpu.make_async_copy(block_ref.at[view], held_ref.at[view], sems.at[n])
        arrivals.append((copy, view))
        first += size
    for copy, _ in arrivals[:2]:
        copy.start()
    rows, group = parts[0].shape
    planes_total = total_ref.shape[0]
    half = planes_total // 2 // group * group
    for n, (copy, view) in enumerate(arrivals):
        copy.wait()
        if n + 2 < len(arrivals):
            arrivals[n + 2][0].start()
        high, low = split(cell_matrix(held_ref.at[view]))
        mixed = nt(high, low * jnp.bfloat16(2))
        total_ref[...] = mixed if n == 0 else total_ref[...] + mixed
        total_ref[:half, :half] += nt(high[:half], high[:half])
        doubled = jnp.concatenate([high[:half] * jnp.bfloat16(2), high[half:]], axis=0)
        total_ref[half:, :] += nt(high[half:], doubled)
    for i in range(planes_total // group):
        for j in range(i + 1):
            here = pl.ds(i * group, group), pl.ds(j * group, group)
            there = pl.ds(j * group, group), pl.ds(i * group, group)
            total_ref[here] = 0.5 * (total_ref[here] + total_ref[there].T)
    my_inner = lax.rem(lax.axis_index("af"), len(parts))
    for place in range(len(parts)):

        @pl.when(my_inner == place)
        def _(place=place):
            for k, part_ref in enumerate(parts):
                start = (place + k) % len(parts) * rows
                copy_rows(part_ref, start, total_ref)


def copy_rows(part_ref, start, total_ref):
    group = part_ref.shape[1]
    half = group // 2
    segments = lower_segments(total_ref.shape[0] // group)

    def quarter(i, skip, size):
        first = i * group
        if first >= total_ref.shape[0]:
            return jnp.zeros((size, half), jnp.float32)
        return total_ref[first + skip : first + skip + size, first : first + half]

    done = 0
    while done < part_ref.shape[0]:
        n, skip = divmod(start + done, half)
        size = min(half - skip, part_ref.shape[0] - done)
        if n >= len(segments):
            value = jnp.zeros((size, group), jnp.float32)
        else:
            i, j, lower = segments[n]
            if i == j and not lower:
                value = jnp.concatenate([quarter(i, skip, size), quarter(i + 1, skip, size)], axis=1)
            else:
                first = i * group + lower * half + skip
                value = total_ref[first : first + size, j * group : (j + 1) * group]
        part_ref[done : done + size, :] = value
        done += size


def gram_pack(block, parts, devices):
    planes_total = block.shape[0] * block.shape[2]
    group = planes_total // largest_step(planes_total, planes_total // 128)
    rows = len(lower_segments(planes_total // group)) * (group // 2)
    rows += -rows % (8 * devices)
    vmem = pl.BlockSpec(memory_space=pltpu.VMEM)
    return pl.pallas_call(
        gram_pack_kernel,
        in_specs=[pl.BlockSpec(memory_space=pl.ANY)],
        out_specs=[vmem] * parts,
        out_shape=[jax.ShapeDtypeStruct((rows // parts, group), jnp.float32)] * parts,
        scratch_shapes=[
            pltpu.VMEM(block.shape, jnp.float32),
            pltpu.VMEM((planes_total, planes_total), jnp.float32),
            pltpu.SemaphoreType.DMA((len(piece_sizes(block.shape[1])),)),
        ],
        compiler_params=pltpu.CompilerParams(vmem_limit_bytes=48 * MIB),
        name="gram_pack",
    )(block)


def inverse_cholesky(matrix):
    size = matrix.shape[0]
    step = largest_step(size, PIVOTS)
    ones = lax.broadcasted_iota(jnp.int32, (size, size), 0) == lax.broadcasted_iota(
        jnp.int32, (size, size), 1
    )
    work = jnp.concatenate([matrix, ones.astype(jnp.float32)], axis=1)
    work = [work[first : first + step] for first in range(0, size, step)]
    shape = work[0].shape
    rows = lax.broadcasted_iota(jnp.int32, shape, 0)
    done = []
    for n in range(len(work)):
        scale = jnp.zeros(shape, jnp.float32)
        columns = {
            m: [
                jnp.broadcast_to(work[m][:, lane : lane + 1], shape)
                for lane in range(n * step, (n + 1) * step)
            ]
            for m in range(n, len(work))
        }
        for i in range(step):
            pivot = columns[n][i][i : i + 1]
            scale = jnp.where(rows == i, lax.rsqrt(pivot), scale)
            inverse = 1.0 / pivot
            row = work[n][i : i + 1] * inverse
            others = [columns[n][k][i : i + 1] * inverse for k in range(i + 1, step)]
            for m in range(n, len(work)):
                factor = columns[m][i]
                if m == n:
                    factor = jnp.where(rows > i, factor, 0.0)
                work[m] = work[m] - factor * row
                for k, other in enumerate(others):
                    columns[m][i + 1 + k] = columns[m][i + 1 + k] - factor * other
        done.append(work[n] * scale)
    return jnp.concatenate(done, axis=0)[:, size:]


def split_three(matrix):
    high, low = split(matrix)
    rest = matrix - high.astype(jnp.float32) - low.astype(jnp.float32)
    return high, low, rest.astype(jnp.bfloat16)


def iterate(matrix, subspace):
    matrix_high, matrix_low, matrix_rest = split_three(matrix)
    rank = subspace.shape[0]
    for _ in range(ITERS):
        high, low, rest = split_three(subspace)
        by_high = nn(jnp.concatenate([high, low, rest], axis=0), matrix_high)
        by_low = nn(jnp.concatenate([high, low], axis=0), matrix_low)
        small = by_high[2 * rank :] + by_low[rank:] + nn(high, matrix_rest)
        product = by_high[:rank] + (by_high[rank : 2 * rank] + by_low[:rank] + small)
        inverse = inverse_cholesky(nt(product, product, HIGHEST))
        subspace = nn(inverse, product, HIGHEST)
    return subspace


def unpack(places, pieces, packed_ref, gram_ref):
    rows, group = pieces[0].shape
    for n, piece in enumerate(pieces):
        packed_ref[pl.ds(pl.multiple_of(places[n] * rows, 8), rows), :] = piece[...]
    half = group // 2
    for n, (i, j, lower) in enumerate(lower_segments(gram_ref.shape[0] // group)):
        segment = packed_ref[n * half : (n + 1) * half, :]
        rows_here = pl.ds(i * group + lower * half, half)
        if i != j:
            gram_ref[rows_here, j * group : (j + 1) * group] = segment
            mirrored = pl.ds(i * group + lower * half, half)
            gram_ref[j * group : (j + 1) * group, mirrored] = segment.T
        elif lower:
            gram_ref[rows_here, i * group : (i + 1) * group] = segment
            gram_ref[i * group : i * group + half, i * group + half : (i + 1) * group] = (
                segment[:, :half].T
            )
        else:
            for k in range(2):
                first = (i + k) * group
                if first < gram_ref.shape[0]:
                    gram_ref[first : first + half, first : first + half] = (
                        segment[:, k * half : (k + 1) * half]
                    )


def finish_kernel(pieces_count, blocks_count, *refs):
    basis_ref = refs[0]
    pieces = refs[1 : 1 + pieces_count]
    blocks = refs[1 + pieces_count : 1 + pieces_count + blocks_count]
    rest = refs[1 + pieces_count + blocks_count :]
    out_ref, packed_ref, gram_ref, result_ref, in_sems, out_sems = rest[:1] + rest[1:4] + rest[-2:]
    held = rest[4:-2]
    steps, first = [], 0
    for n, block in enumerate(blocks):
        for start in range(0, block.shape[1], PROJECT_CELLS):
            size = min(PROJECT_CELLS, block.shape[1] - start)
            cells = (slice(None), pl.ds(start, size))
            copy = pltpu.make_async_copy(
                block.at[cells], held[n].at[cells], in_sems.at[len(steps)]
            )
            copy.start()
            steps.append((held[n].at[cells], pl.ds(first, size), copy))
            first += size
    unpack(piece_places(), pieces, packed_ref, gram_ref)
    subspace = iterate(gram_ref[...], basis_ref[...])
    rank = subspace.shape[0]
    basis_high, basis_low = split(subspace)
    both = jnp.concatenate([basis_high, basis_low], axis=0)
    copies = []
    for n, (block, cells, arrival) in enumerate(steps):
        arrival.wait()
        cells_y = block.shape[3]
        high, low = split(cell_matrix(block))
        main = nn(both, high)
        result = main[:rank] + (main[rank:] + nn(basis_high, low))
        for i in range(cells.size):
            result_ref[cells.start + i] = result[:, i * cells_y : (i + 1) * cells_y]
        copy = pltpu.make_async_copy(result_ref.at[cells], out_ref.at[cells], out_sems.at[n])
        copy.start()
        copies.append(copy)
    for copy in copies:
        copy.wait()


def finish(pieces, basis_t, blocks):
    rank, planes_total = basis_t.shape
    cells = sum(block.shape[1] for block in blocks)
    cells_y = blocks[0].shape[3]
    rows, group = pieces[0].shape
    steps = sum(pl.cdiv(block.shape[1], PROJECT_CELLS) for block in blocks)
    vmem = pl.BlockSpec(memory_space=pltpu.VMEM)
    anywhere = pl.BlockSpec(memory_space=pl.ANY)
    out_shape = (cells, rank, cells_y)
    return pl.pallas_call(
        functools.partial(finish_kernel, len(pieces), len(blocks)),
        in_specs=[vmem] * (1 + len(pieces))
        + [anywhere] * len(blocks),
        out_specs=anywhere,
        out_shape=jax.ShapeDtypeStruct(out_shape, jnp.float32),
        scratch_shapes=[
            pltpu.VMEM((rows * len(pieces), group), jnp.float32),
            pltpu.VMEM((planes_total, planes_total), jnp.float32),
            pltpu.VMEM(out_shape, jnp.float32),
        ]
        + [pltpu.VMEM(block.shape, jnp.float32) for block in blocks]
        + [pltpu.SemaphoreType.DMA((steps,)), pltpu.SemaphoreType.DMA((steps,))],
        compiler_params=pltpu.CompilerParams(vmem_limit_bytes=56 * MIB),
        name="finish",
    )(basis_t, *pieces, *blocks)


def toward(i, step, count):
    return i ^ step if count & (count - 1) == 0 else (i + step) % count


def origin(i, step, count):
    return i ^ step if count & (count - 1) == 0 else (i - step) % count


def inner_size():
    return 2 if lax.axis_size("af") % 2 == 0 else 1


def af_place():
    inner = inner_size()
    me = lax.axis_index("af")
    return lax.div(me, inner), lax.rem(me, inner), lax.axis_size("af") // inner


def piece_places():
    my_outer, my_inner, outer = af_place()
    places = []
    for i in range(inner_size()):
        group = my_inner if i == 0 else 1 - my_inner
        places += [group * outer + origin(my_outer, k, outer) for k in range(outer)]
    return places


def cut_kernel(kept_ref, came_ref, *refs):
    outs, total_ref = refs[:-1], refs[-1]
    my_outer, _, outer = af_place()
    total_ref[...] = kept_ref[...] + came_ref[...]
    rows = outs[0].shape[0]
    for k, out_ref in enumerate(outs):
        start = toward(my_outer, k, outer) * rows
        out_ref[...] = total_ref[pl.ds(pl.multiple_of(start, 8), rows), :]


def cut(kept, came, outer):
    rows, group = kept.shape
    vmem = pl.BlockSpec(memory_space=pltpu.VMEM)
    return pl.pallas_call(
        cut_kernel,
        in_specs=[vmem] * 2,
        out_specs=[vmem] * outer,
        out_shape=[jax.ShapeDtypeStruct((rows // outer, group), jnp.float32)] * outer,
        scratch_shapes=[pltpu.VMEM(kept.shape, jnp.float32)],
        compiler_params=pltpu.CompilerParams(vmem_limit_bytes=8 * MIB),
        name="cut",
    )(kept, came)


def sum_over_devices(parts):
    groups_af, groups_ta = lax.axis_size("af"), lax.axis_size("ta")
    inner = inner_size()
    outer = groups_af // inner

    def to_inner(array):
        return lax.ppermute(array, "af", [(i, i ^ 1) for i in range(groups_af)])

    def to_outer(array, step):
        return lax.ppermute(
            array,
            "af",
            [(i, toward(i // inner, step, outer) * inner + i % inner) for i in range(groups_af)],
        )

    def to_ta(array, step):
        return lax.ppermute(array, "ta", [(i, toward(i, step, groups_ta)) for i in range(groups_ta)])

    def total(arrays):
        return functools.reduce(jnp.add, arrays)

    came = to_inner(parts[1]) if inner == 2 else jnp.zeros_like(parts[0])
    parts = cut(parts[0], came, outer)
    mine = total([parts[0]] + [to_outer(parts[k], k) for k in range(1, outer)])
    mine = total([mine] + [to_ta(mine, k) for k in range(1, groups_ta)])
    pieces = [mine] + [to_outer(mine, k) for k in range(1, outer)]
    if inner == 2:
        pieces += [to_inner(piece) for piece in pieces]
    return pieces


def arrange_kernel(spots, in_ref, out_ref, held_ref, sems):
    part, targets = held_ref.shape[3], held_ref.shape[2]
    arrivals = []
    for n, (frame, x, _, _) in enumerate(spots):
        copy = pltpu.make_async_copy(
            in_ref.at[frame, :, :, pl.ds(x, part)], held_ref.at[n], sems.at[n]
        )
        copy.start()
        arrivals.append(copy)
    for n, (_, _, group, cell) in enumerate(spots):
        arrivals[n].wait()
        for target in range(targets):
            out_ref[group * targets + target, cell : cell + part] = jnp.swapaxes(
                held_ref[n, :, target], 0, 1
            )


def outgoing(velocity):
    groups_ta, groups_af = lax.axis_size("ta"), lax.axis_size("af")
    frames, planes, cells_x, cells_y = velocity.shape
    block_frames, block_x = frames // groups_ta, cells_x // groups_af
    cells = block_frames * block_x
    if planes % 8 or block_x % 8:
        ordered = velocity.reshape(groups_ta, block_frames, planes, groups_af, block_x, cells_y)
        ordered = ordered.transpose(0, 3, 1, 4, 2, 5)
        return ordered.reshape(groups_ta * groups_af, cells, planes, cells_y)
    spots = [
        (group * block_frames + frame, 0, group, frame * block_x)
        for group in range(groups_ta)
        for frame in range(block_frames)
    ]
    anywhere = pl.BlockSpec(memory_space=pl.ANY)
    return pl.pallas_call(
        functools.partial(arrange_kernel, spots),
        in_specs=[anywhere],
        out_specs=pl.BlockSpec(memory_space=pltpu.VMEM),
        out_shape=jax.ShapeDtypeStruct(
            (groups_ta * groups_af, cells, planes, cells_y), jnp.float32
        ),
        scratch_shapes=[
            pltpu.VMEM((len(spots), planes, groups_af, block_x, cells_y), jnp.float32),
            pltpu.SemaphoreType.DMA((len(spots),)),
        ],
        compiler_params=pltpu.CompilerParams(vmem_limit_bytes=30 * MIB),
        name="arrange",
    )(velocity.reshape(frames, planes, groups_af, block_x, cells_y))


def local(velocity, initial_basis):
    groups_ta, groups_af = lax.axis_size("ta"), lax.axis_size("af")
    frames, planes, cells_x, cells_y = velocity.shape
    block_frames, block_x = frames // groups_ta, cells_x // groups_af
    block = lax.all_to_all(
        outgoing(velocity), ("ta", "af"), split_axis=0, concat_axis=0, tiled=True
    )
    if planes % 8:
        block = block.transpose(1, 0, 2, 3).reshape(1, block.shape[1], -1, cells_y)
    inner = inner_size()
    pieces = sum_over_devices(gram_pack(block, inner, groups_af))
    core = finish(pieces, initial_basis.T, [block])
    return core.reshape(block_frames, block_x, core.shape[1], cells_y)


def solution(mesh):
    placed = (P(None, ("ta", "af"), None, None), P())
    return jax.shard_map(
        local, mesh=mesh, in_specs=placed, out_specs=P("ta", "af", None, None), check_vma=False
    )
```

```python
import functools

import jax
import jax.numpy as jnp
from jax import lax
from jax.experimental import pallas as pl
from jax.experimental.pallas import tpu as pltpu
from jax.sharding import PartitionSpec as P

ITERS = 3
HIGHEST = lax.Precision.HIGHEST
MIB = 1024 * 1024
PIVOTS = 16
PROJECT_CELLS = 16


def split(matrix):
    high = matrix.astype(jnp.bfloat16)
    low = (matrix - high.astype(jnp.float32)).astype(jnp.bfloat16)
    return high, low


def nn(left, right, precision=None):
    return lax.dot_general(
        left, right, (((1,), (0,)), ((), ())), precision=precision,
        preferred_element_type=jnp.float32,
    )


def nt(left, right, precision=None):
    return lax.dot_general(
        left, right, (((1,), (1,)), ((), ())), precision=precision,
        preferred_element_type=jnp.float32,
    )


def largest_step(extent, most):
    step = min(extent, most)
    while extent % step:
        step -= 1
    return step


def cell_matrix(block_ref):
    sources, cells, planes, cells_y = block_ref.shape
    return jnp.concatenate(
        [block_ref[:, i].reshape(sources * planes, cells_y) for i in range(cells)], axis=1
    )


def lower_segments(count):
    below = [(i, j, half) for i in range(count) for j in range(i) for half in range(2)]
    return below + [(i, i, 1) for i in range(count)] + [(i, i, 0) for i in range(0, count, 2)]


def piece_sizes(cells):
    sizes, size = [], 4
    while cells:
        sizes.append(min(size, cells))
        cells -= sizes[-1]
        size = min(3 * size, 24)
    return sizes


def gram_pack_kernel(block_ref, *refs):
    parts, held_ref, total_ref, sems = refs[:-3], refs[-3], refs[-2], refs[-1]
    arrivals, first = [], 0
    for n, size in enumerate(piece_sizes(block_ref.shape[1])):
        view = (slice(None), pl.ds(first, size))
        copy = pltpu.make_async_copy(block_ref.at[view], held_ref.at[view], sems.at[n])
        copy.start()
        arrivals.append((copy, view))
        first += size
    rows, group = parts[0].shape
    planes_total = total_ref.shape[0]
    half = planes_total // 2 // group * group
    for n, (copy, view) in enumerate(arrivals):
        copy.wait()
        high, low = split(cell_matrix(held_ref.at[view]))
        mixed = nt(high, low * jnp.bfloat16(2))
        total_ref[...] = mixed if n == 0 else total_ref[...] + mixed
        total_ref[:half, :half] += nt(high[:half], high[:half])
        doubled = jnp.concatenate([high[:half] * jnp.bfloat16(2), high[half:]], axis=0)
        total_ref[half:, :] += nt(high[half:], doubled)
    for i in range(planes_total // group):
        for j in range(i + 1):
            here = pl.ds(i * group, group), pl.ds(j * group, group)
            there = pl.ds(j * group, group), pl.ds(i * group, group)
            total_ref[here] = 0.5 * (total_ref[here] + total_ref[there].T)
    my_inner = lax.rem(lax.axis_index("af"), len(parts))
    for place in range(len(parts)):

        @pl.when(my_inner == place)
        def _(place=place):
            for k, part_ref in enumerate(parts):
                start = (place + k) % len(parts) * rows
                copy_rows(part_ref, start, total_ref)


def copy_rows(part_ref, start, total_ref):
    group = part_ref.shape[1]
    half = group // 2
    segments = lower_segments(total_ref.shape[0] // group)

    def quarter(i, skip, size):
        first = i * group
        if first >= total_ref.shape[0]:
            return jnp.zeros((size, half), jnp.float32)
        return total_ref[first + skip : first + skip + size, first : first + half]

    done = 0
    while done < part_ref.shape[0]:
        n, skip = divmod(start + done, half)
        size = min(half - skip, part_ref.shape[0] - done)
        if n >= len(segments):
            value = jnp.zeros((size, group), jnp.float32)
        else:
            i, j, lower = segments[n]
            if i == j and not lower:
                value = jnp.concatenate([quarter(i, skip, size), quarter(i + 1, skip, size)], axis=1)
            else:
                first = i * group + lower * half + skip
                value = total_ref[first : first + size, j * group : (j + 1) * group]
        part_ref[done : done + size, :] = value
        done += size


def gram_pack(block, parts, devices):
    planes_total = block.shape[0] * block.shape[2]
    group = planes_total // largest_step(planes_total, planes_total // 128)
    rows = len(lower_segments(planes_total // group)) * (group // 2)
    rows += -rows % (8 * devices)
    vmem = pl.BlockSpec(memory_space=pltpu.VMEM)
    return pl.pallas_call(
        gram_pack_kernel,
        in_specs=[pl.BlockSpec(memory_space=pl.ANY)],
        out_specs=[vmem] * parts,
        out_shape=[jax.ShapeDtypeStruct((rows // parts, group), jnp.float32)] * parts,
        scratch_shapes=[
            pltpu.VMEM(block.shape, jnp.float32),
            pltpu.VMEM((planes_total, planes_total), jnp.float32),
            pltpu.SemaphoreType.DMA((len(piece_sizes(block.shape[1])),)),
        ],
        compiler_params=pltpu.CompilerParams(vmem_limit_bytes=48 * MIB),
        name="gram_pack",
    )(block)


def inverse_cholesky(matrix):
    size = matrix.shape[0]
    step = largest_step(size, PIVOTS)
    ones = lax.broadcasted_iota(jnp.int32, (size, size), 0) == lax.broadcasted_iota(
        jnp.int32, (size, size), 1
    )
    work = jnp.concatenate([matrix, ones.astype(jnp.float32)], axis=1)
    work = [work[first : first + step] for first in range(0, size, step)]
    shape = work[0].shape
    rows = lax.broadcasted_iota(jnp.int32, shape, 0)
    done = []
    for n in range(len(work)):
        scale = jnp.zeros(shape, jnp.float32)
        columns = {
            m: [
                jnp.broadcast_to(work[m][:, lane : lane + 1], shape)
                for lane in range(n * step, (n + 1) * step)
            ]
            for m in range(n, len(work))
        }
        for i in range(step):
            pivot = columns[n][i][i : i + 1]
            scale = jnp.where(rows == i, lax.rsqrt(pivot), scale)
            inverse = 1.0 / pivot
            row = work[n][i : i + 1] * inverse
            others = [columns[n][k][i : i + 1] * inverse for k in range(i + 1, step)]
            for m in range(n, len(work)):
                factor = columns[m][i]
                if m == n:
                    factor = jnp.where(rows > i, factor, 0.0)
                work[m] = work[m] - factor * row
                for k, other in enumerate(others):
                    columns[m][i + 1 + k] = columns[m][i + 1 + k] - factor * other
        done.append(work[n] * scale)
    return jnp.concatenate(done, axis=0)[:, size:]


def split_three(matrix):
    high, low = split(matrix)
    rest = matrix - high.astype(jnp.float32) - low.astype(jnp.float32)
    return high, low, rest.astype(jnp.bfloat16)


def iterate(matrix, subspace):
    matrix_high, matrix_low, matrix_rest = split_three(matrix)
    rank = subspace.shape[0]
    for _ in range(ITERS):
        high, low, rest = split_three(subspace)
        by_high = nn(jnp.concatenate([high, low, rest], axis=0), matrix_high)
        by_low = nn(jnp.concatenate([high, low], axis=0), matrix_low)
        small = by_high[2 * rank :] + by_low[rank:] + nn(high, matrix_rest)
        product = by_high[:rank] + (by_high[rank : 2 * rank] + by_low[:rank] + small)
        inverse = inverse_cholesky(nt(product, product, HIGHEST))
        subspace = nn(inverse, product, HIGHEST)
    return subspace


def unpack(places, pieces, packed_ref, gram_ref):
    rows, group = pieces[0].shape
    for n, piece in enumerate(pieces):
        packed_ref[pl.ds(pl.multiple_of(places[n] * rows, 8), rows), :] = piece[...]
    half = group // 2
    for n, (i, j, lower) in enumerate(lower_segments(gram_ref.shape[0] // group)):
        segment = packed_ref[n * half : (n + 1) * half, :]
        rows_here = pl.ds(i * group + lower * half, half)
        if i != j:
            gram_ref[rows_here, j * group : (j + 1) * group] = segment
            mirrored = pl.ds(i * group + lower * half, half)
            gram_ref[j * group : (j + 1) * group, mirrored] = segment.T
        elif lower:
            gram_ref[rows_here, i * group : (i + 1) * group] = segment
            gram_ref[i * group : i * group + half, i * group + half : (i + 1) * group] = (
                segment[:, :half].T
            )
        else:
            for k in range(2):
                first = (i + k) * group
                if first < gram_ref.shape[0]:
                    gram_ref[first : first + half, first : first + half] = (
                        segment[:, k * half : (k + 1) * half]
                    )


def finish_kernel(pieces_count, blocks_count, *refs):
    basis_ref = refs[0]
    pieces = refs[1 : 1 + pieces_count]
    blocks = refs[1 + pieces_count : 1 + pieces_count + blocks_count]
    rest = refs[1 + pieces_count + blocks_count :]
    out_ref, packed_ref, gram_ref, result_ref, in_sems, out_sems = rest[:1] + rest[1:4] + rest[-2:]
    held = rest[4:-2]
    steps, first = [], 0
    for n, block in enumerate(blocks):
        for start in range(0, block.shape[1], PROJECT_CELLS):
            size = min(PROJECT_CELLS, block.shape[1] - start)
            cells = (slice(None), pl.ds(start, size))
            copy = pltpu.make_async_copy(
                block.at[cells], held[n].at[cells], in_sems.at[len(steps)]
            )
            copy.start()
            steps.append((held[n].at[cells], pl.ds(first, size), copy))
            first += size
    unpack(piece_places(), pieces, packed_ref, gram_ref)
    subspace = iterate(gram_ref[...], basis_ref[...])
    rank = subspace.shape[0]
    basis_high, basis_low = split(subspace)
    both = jnp.concatenate([basis_high, basis_low], axis=0)
    copies = []
    for n, (block, cells, arrival) in enumerate(steps):
        arrival.wait()
        cells_y = block.shape[3]
        high, low = split(cell_matrix(block))
        main = nn(both, high)
        result = main[:rank] + (main[rank:] + nn(basis_high, low))
        for i in range(cells.size):
            result_ref[cells.start + i] = result[:, i * cells_y : (i + 1) * cells_y]
        copy = pltpu.make_async_copy(result_ref.at[cells], out_ref.at[cells], out_sems.at[n])
        copy.start()
        copies.append(copy)
    for copy in copies:
        copy.wait()


def finish(pieces, basis_t, blocks):
    rank, planes_total = basis_t.shape
    cells = sum(block.shape[1] for block in blocks)
    cells_y = blocks[0].shape[3]
    rows, group = pieces[0].shape
    steps = sum(pl.cdiv(block.shape[1], PROJECT_CELLS) for block in blocks)
    vmem = pl.BlockSpec(memory_space=pltpu.VMEM)
    anywhere = pl.BlockSpec(memory_space=pl.ANY)
    out_shape = (cells, rank, cells_y)
    return pl.pallas_call(
        functools.partial(finish_kernel, len(pieces), len(blocks)),
        in_specs=[vmem] * (1 + len(pieces))
        + [anywhere] * len(blocks),
        out_specs=anywhere,
        out_shape=jax.ShapeDtypeStruct(out_shape, jnp.float32),
        scratch_shapes=[
            pltpu.VMEM((rows * len(pieces), group), jnp.float32),
            pltpu.VMEM((planes_total, planes_total), jnp.float32),
            pltpu.VMEM(out_shape, jnp.float32),
        ]
        + [pltpu.VMEM(block.shape, jnp.float32) for block in blocks]
        + [pltpu.SemaphoreType.DMA((steps,)), pltpu.SemaphoreType.DMA((steps,))],
        compiler_params=pltpu.CompilerParams(vmem_limit_bytes=56 * MIB),
        name="finish",
    )(basis_t, *pieces, *blocks)


def toward(i, step, count):
    return i ^ step if count & (count - 1) == 0 else (i + step) % count


def origin(i, step, count):
    return i ^ step if count & (count - 1) == 0 else (i - step) % count


def inner_size():
    return 2 if lax.axis_size("af") % 2 == 0 else 1


def af_place():
    inner = inner_size()
    me = lax.axis_index("af")
    return lax.div(me, inner), lax.rem(me, inner), lax.axis_size("af") // inner


def piece_places():
    my_outer, my_inner, outer = af_place()
    places = []
    for i in range(inner_size()):
        group = my_inner if i == 0 else 1 - my_inner
        places += [group * outer + origin(my_outer, k, outer) for k in range(outer)]
    return places


def cut_kernel(kept_ref, came_ref, *refs):
    outs, total_ref = refs[:-1], refs[-1]
    my_outer, _, outer = af_place()
    total_ref[...] = kept_ref[...] + came_ref[...]
    rows = outs[0].shape[0]
    for k, out_ref in enumerate(outs):
        start = toward(my_outer, k, outer) * rows
        out_ref[...] = total_ref[pl.ds(pl.multiple_of(start, 8), rows), :]


def cut(kept, came, outer):
    rows, group = kept.shape
    vmem = pl.BlockSpec(memory_space=pltpu.VMEM)
    return pl.pallas_call(
        cut_kernel,
        in_specs=[vmem] * 2,
        out_specs=[vmem] * outer,
        out_shape=[jax.ShapeDtypeStruct((rows // outer, group), jnp.float32)] * outer,
        scratch_shapes=[pltpu.VMEM(kept.shape, jnp.float32)],
        compiler_params=pltpu.CompilerParams(vmem_limit_bytes=8 * MIB),
        name="cut",
    )(kept, came)


def sum_over_devices(parts):
    groups_af, groups_ta = lax.axis_size("af"), lax.axis_size("ta")
    inner = inner_size()
    outer = groups_af // inner

    def to_inner(array):
        return lax.ppermute(array, "af", [(i, i ^ 1) for i in range(groups_af)])

    def to_outer(array, step):
        return lax.ppermute(
            array,
            "af",
            [(i, toward(i // inner, step, outer) * inner + i % inner) for i in range(groups_af)],
        )

    def to_ta(array, step):
        return lax.ppermute(array, "ta", [(i, toward(i, step, groups_ta)) for i in range(groups_ta)])

    def total(arrays):
        return functools.reduce(jnp.add, arrays)

    came = to_inner(parts[1]) if inner == 2 else jnp.zeros_like(parts[0])
    parts = cut(parts[0], came, outer)
    mine = total([parts[0]] + [to_outer(parts[k], k) for k in range(1, outer)])
    mine = total([mine] + [to_ta(mine, k) for k in range(1, groups_ta)])
    pieces = [mine] + [to_outer(mine, k) for k in range(1, outer)]
    if inner == 2:
        pieces += [to_inner(piece) for piece in pieces]
    return pieces


def arrange_kernel(spots, in_ref, out_ref, held_ref, sems):
    part, targets = held_ref.shape[3], held_ref.shape[2]
    arrivals = []
    for n, (frame, x, _, _) in enumerate(spots):
        copy = pltpu.make_async_copy(
            in_ref.at[frame, :, :, pl.ds(x, part)], held_ref.at[n], sems.at[n]
        )
        copy.start()
        arrivals.append(copy)
    for n, (_, _, group, cell) in enumerate(spots):
        arrivals[n].wait()
        for target in range(targets):
            out_ref[group * targets + target, cell : cell + part] = jnp.swapaxes(
                held_ref[n, :, target], 0, 1
            )


def outgoing(velocity):
    groups_ta, groups_af = lax.axis_size("ta"), lax.axis_size("af")
    frames, planes, cells_x, cells_y = velocity.shape
    block_frames, block_x = frames // groups_ta, cells_x // groups_af
    cells = block_frames * block_x
    if planes % 8 or block_x % 8:
        ordered = velocity.reshape(groups_ta, block_frames, planes, groups_af, block_x, cells_y)
        ordered = ordered.transpose(0, 3, 1, 4, 2, 5)
        return ordered.reshape(groups_ta * groups_af, cells, planes, cells_y)
    spots = [
        (group * block_frames + frame, 0, group, frame * block_x)
        for group in range(groups_ta)
        for frame in range(block_frames)
    ]
    anywhere = pl.BlockSpec(memory_space=pl.ANY)
    return pl.pallas_call(
        functools.partial(arrange_kernel, spots),
        in_specs=[anywhere],
        out_specs=pl.BlockSpec(memory_space=pltpu.VMEM),
        out_shape=jax.ShapeDtypeStruct(
            (groups_ta * groups_af, cells, planes, cells_y), jnp.float32
        ),
        scratch_shapes=[
            pltpu.VMEM((len(spots), planes, groups_af, block_x, cells_y), jnp.float32),
            pltpu.SemaphoreType.DMA((len(spots),)),
        ],
        compiler_params=pltpu.CompilerParams(vmem_limit_bytes=30 * MIB),
        name="arrange",
    )(velocity.reshape(frames, planes, groups_af, block_x, cells_y))


def local(velocity, initial_basis):
    groups_ta, groups_af = lax.axis_size("ta"), lax.axis_size("af")
    frames, planes, cells_x, cells_y = velocity.shape
    block_frames, block_x = frames // groups_ta, cells_x // groups_af
    block = lax.all_to_all(
        outgoing(velocity), ("ta", "af"), split_axis=0, concat_axis=0, tiled=True
    )
    if planes % 8:
        block = block.transpose(1, 0, 2, 3).reshape(1, block.shape[1], -1, cells_y)
    inner = inner_size()
    pieces = sum_over_devices(gram_pack(block, inner, groups_af))
    core = finish(pieces, initial_basis.T, [block])
    return core.reshape(block_frames, block_x, core.shape[1], cells_y)


def solution(mesh):
    placed = (P(None, ("ta", "af"), None, None), P())
    return jax.shard_map(
        local, mesh=mesh, in_specs=placed, out_specs=P("ta", "af", None, None), check_vma=False
    )
```
